128 devices in a mesh: pool: 4 (over y), tp: 32 (over x, z, core).
Axes of the slice: x: 4, y: 4, z: 4, core: 2. Of those that a mesh axis runs over, the one named last changes fastest.
Arguments:
- tokens: bfloat16 [2048, 8192], P('pool', 'tp'), may hold values from -6 to 6
- w_query: bfloat16 [8192, 8192], P(None, 'tp'), may hold values from -0.0625 to 0.0625
- w_key: bfloat16 [8192, 8192], P(None, 'tp'), may hold values from -0.0625 to 0.0625
- w_value: bfloat16 [8192, 8192], P(None, 'tp'), may hold values from -0.0625 to 0.0625
- w_gate: bfloat16 [8192, 8192], P(None, 'tp'), may hold values from -0.0625 to 0.0625
- decay: float32 [32], P('tp'), as said below
- pool_states: float32 [32, 32, 256, 256], P('pool', 'tp'), may hold values from -0.75 to 0.75
- lengths: int32 [32], replicated, may hold values from 1 to 128, as said below
- slot_of: int32 [32], replicated, may hold values from 0 to 31, as said below
- serve: int32 [32], replicated, may hold values from 0 to 3, as said below
Outputs:
- retained: bfloat16 [2048, 8192], P('pool', 'tp')
- new_states: float32 [32, 32, 256, 256], P('pool', 'tp')
The draws below stay inside these ranges and needn't reach their ends.
Inputs may be any that keep to these rules, and one draw needn't show every extreme that they name: `lengths`: each turn has 1 to 128 tokens and some turn exactly 128. The turns served by one group total at most 512 tokens; one group serves exactly 16 sessions whose turns total exactly 512. A permutation of the pool rows; the owner group of session s is slot_of[s] // 8. At most 4 sessions of one owner group are served by one group, and exactly 4 for some pairs of groups. `serve`: A group's turns are packed in increasing session order from the first row of its block of 512 rows; the remaining rows are padding. `decay`: between 0 and 1 for every head.
All inputs are finite; a program needn't handle non-finite values.
Results may differ from the reference program's by a relative error of at most 0.014.
Values may be sent and summed in bfloat16 or wider, within the bound.
A program may use at most 128 MiB of HBM per device.

```python
import math
import jax
import jax.numpy as jnp
from jax import lax

D = 8192
HEADS = 32
HEAD = 256
VHEAD = 256
SESSIONS = 32
LMAX = 128
CAP = 512
ROWS = 2048
HD = 8192
VD = 8192
N_POOL = 4


def turn_lengths(key, count):
    key_wobble, key_place = jax.random.split(key)
    rest_count = count - 1
    remain = CAP - LMAX
    typical = remain // rest_count
    extra = remain % rest_count
    baseline = typical + (jnp.arange(rest_count, dtype=jnp.int32) < extra).astype(jnp.int32)
    pair_count = rest_count // 2
    wobble = jax.random.randint(key_wobble, (pair_count,), -(typical - 1), typical).astype(jnp.int32)
    shifted = jnp.concatenate([wobble, -wobble, jnp.zeros((rest_count - 2 * pair_count,), jnp.int32)])
    values = jnp.concatenate([jnp.array([LMAX], jnp.int32), baseline + shifted])
    return values[jax.random.permutation(key_place, count)]


def session_plan(key):
    keys_all = jax.random.split(key, 6)
    half_count = SESSIONS // 2
    per_owner = SESSIONS // (2 * N_POOL)
    owned = SESSIONS // N_POOL
    session_order = jax.random.permutation(keys_all[0], SESSIONS).astype(jnp.int32)
    busiest = jax.random.randint(keys_all[1], (), 0, N_POOL)
    position = jnp.arange(SESSIONS, dtype=jnp.int32)
    others = (busiest + 1 + jax.random.randint(keys_all[2], (SESSIONS,), 0, N_POOL - 1)) % N_POOL
    in_busy = position < half_count
    served = jnp.where(in_busy, busiest, others).astype(jnp.int32)
    within_half = position % half_count
    owner_group = within_half % N_POOL
    within = within_half // N_POOL + jnp.where(in_busy, 0, per_owner)
    shuffle = jnp.stack([jax.random.permutation(sub_key, owned) for sub_key in jax.random.split(keys_all[3], N_POOL)])
    pool_row = (owner_group * owned + shuffle[owner_group, within]).astype(jnp.int32)
    turn_all = jnp.concatenate([turn_lengths(keys_all[4], half_count), turn_lengths(keys_all[5], half_count)])
    inverse = jnp.argsort(session_order)
    return (turn_all[inverse].astype(jnp.int32), pool_row[inverse], served[inverse])


def draw_lengths(key, part):
    return session_plan(key)[0]


def draw_slot_of(key, part):
    return session_plan(key)[1]


def draw_serve(key, part):
    return session_plan(key)[2]


def draw_decay(key, part):
    key = jax.random.fold_in(key, 11)
    spread = jax.random.uniform(key, (HEADS,), jnp.float32)
    lowest = math.log(1.0 / 600.0)
    highest = math.log(1.0 / 24.0)
    return 1.0 - jnp.exp(lowest + spread * (highest - lowest))


def block_scale(own_key, extent, cuts, smallest, top_value):
    gain = 1.0
    for axis_at, parts in cuts:
        draws = jax.random.uniform(jax.random.fold_in(jax.random.fold_in(own_key, 6), axis_at), (parts,), jnp.float32, smallest / len(cuts), top_value / len(cuts))
        gain = gain * jnp.repeat(jnp.exp(draws), extent[axis_at] // parts).reshape((-1,) + (1,) * (len(extent) - 1 - axis_at))
    return gain


def normal_values(stream_key, extent, deviation, bound, cuts=(), held_as=jnp.bfloat16):
    drawn = deviation * jax.random.normal(stream_key, extent, jnp.float32)
    if cuts:
        drawn = drawn * block_scale(stream_key, extent, cuts, -0.22, 0.18)
    return jnp.clip(drawn, -bound, bound).astype(held_as)


def setup_inputs(seed: int = 0) -> dict:
    arg_keys = jax.random.split(jax.random.key(seed), 11)
    tokens = normal_values(arg_keys[0], (ROWS, D), 1.0, 6.0, ((0, 4), (1, 32)))
    w_query = normal_values(arg_keys[1], (D, HD), D ** -0.5, 0.0625, ((1, 32),))
    w_key = normal_values(arg_keys[2], (D, HD), D ** -0.5, 0.0625, ((1, 32),))
    w_value = normal_values(arg_keys[3], (D, VD), D ** -0.5, 0.0625, ((1, 32),))
    w_gate = normal_values(arg_keys[4], (D, VD), D ** -0.5, 0.0625, ((1, 32),))
    decay = draw_decay(jax.random.fold_in(arg_keys[10], 71), 0)
    pool_states = normal_values(arg_keys[6], (SESSIONS, HEADS, HEAD, VHEAD), 0.125, 0.75, ((0, 4), (1, 32)), jnp.float32)
    lengths = draw_lengths(jax.random.fold_in(arg_keys[10], 71), 0)
    slot_of = draw_slot_of(jax.random.fold_in(arg_keys[10], 71), 0)
    serve = draw_serve(jax.random.fold_in(arg_keys[10], 71), 0)
    return {"tokens": tokens, "w_query": w_query, "w_key": w_key, "w_value": w_value, "w_gate": w_gate, "decay": decay, "pool_states": pool_states, "lengths": lengths, "slot_of": slot_of, "serve": serve}


norm_epsilon = 1e-05

def reference(tokens, w_query, w_key, w_value, w_gate, decay, pool_states, lengths, slot_of, serve):
    query = jnp.dot(tokens, w_query, preferred_element_type=jnp.float32).astype(jnp.bfloat16)
    keys = (jnp.dot(tokens, w_key, preferred_element_type=jnp.float32) * HEAD ** (-0.5)).astype(jnp.bfloat16)
    values = jnp.dot(tokens, w_value, preferred_element_type=jnp.float32).astype(jnp.bfloat16)
    gate = jnp.dot(tokens, w_gate, preferred_element_type=jnp.float32).astype(jnp.bfloat16)
    row_total = N_POOL * CAP
    session_ids = jnp.arange(SESSIONS, dtype=jnp.int32)
    same_group = serve[:, None] == serve[None, :]
    earlier = lax.optimization_barrier(jnp.sum(jnp.where(same_group & (session_ids[None, :] < session_ids[:, None]), lengths[None, :], 0), axis=1))
    base = (serve * CAP + earlier).astype(jnp.int32)
    row_index = jnp.arange(row_total, dtype=jnp.int32)
    inside = ((row_index[:, None] >= base[None, :]) & (row_index[:, None] < (base + lengths)[None, :])).astype(jnp.int32)
    is_live = lax.optimization_barrier(jnp.sum(inside, axis=1)) > 0
    turn_id = jnp.where(is_live, lax.optimization_barrier(jnp.sum(inside * session_ids[None, :], axis=1)), -1)
    position = row_index - lax.optimization_barrier(jnp.sum(inside * base[None, :], axis=1))
    log_gamma = jnp.log(decay)
    query_heads = query.reshape(row_total, HEADS, HEAD)
    key_heads = keys.reshape(row_total, HEADS, HEAD)
    value_heads = values.reshape(row_total, HEADS, VHEAD)
    blocks = []
    for block_group in range(N_POOL):
        low_row = block_group * CAP
        block_ids = turn_id[low_row:low_row + CAP]
        block_rows = row_index[low_row:low_row + CAP]
        block_pos = position[low_row:low_row + CAP]
        same_turn = (block_ids[:, None] == block_ids[None, :]) & (block_ids[:, None] >= 0) & (block_rows[None, :] <= block_rows[:, None])
        distance = (block_pos[:, None] - block_pos[None, :]).astype(jnp.float32)

        def one_head(packed, same_turn=same_turn, distance=distance):
            head_query, head_keys, head_values, head_log = packed
            scores = jnp.dot(head_query, head_keys.T, preferred_element_type=jnp.float32)
            weight = jnp.where(same_turn, jnp.exp(jnp.maximum(distance, 0.0) * head_log), 0.0)
            mixing = (scores * weight).astype(jnp.bfloat16)
            return jnp.dot(mixing, head_values, preferred_element_type=jnp.float32)
        result = lax.map(one_head, (query_heads[low_row:low_row + CAP].transpose(1, 0, 2), key_heads[low_row:low_row + CAP].transpose(1, 0, 2), value_heads[low_row:low_row + CAP].transpose(1, 0, 2), log_gamma))
        blocks.append(result.transpose(1, 0, 2))
    inside_sum = jnp.concatenate(blocks, axis=0)
    query_pad = jnp.concatenate([query_heads, jnp.zeros((LMAX, HEADS, HEAD), jnp.bfloat16)], axis=0)
    key_pad = jnp.concatenate([key_heads, jnp.zeros((LMAX, HEADS, HEAD), jnp.bfloat16)], axis=0)
    value_pad = jnp.concatenate([value_heads, jnp.zeros((LMAX, HEADS, VHEAD), jnp.bfloat16)], axis=0)
    offsets = jnp.arange(LMAX, dtype=jnp.int32)

    def visit_session(session, carry):
        carried, updated = carry
        first_row = base[session].astype(jnp.int32)
        turn_len = lengths[session]
        pool_row = slot_of[session].astype(jnp.int32)
        query_rows = lax.dynamic_slice_in_dim(query_pad, first_row, LMAX, 0).astype(jnp.float32)
        key_rows = lax.dynamic_slice_in_dim(key_pad, first_row, LMAX, 0).astype(jnp.float32)
        value_rows = lax.dynamic_slice_in_dim(value_pad, first_row, LMAX, 0).astype(jnp.float32)
        prior_state = lax.dynamic_index_in_dim(pool_states, pool_row, 0, keepdims=False)
        in_turn = offsets < turn_len
        reach_decay = jnp.where(in_turn[:, None], jnp.exp((offsets[:, None] + 1).astype(jnp.float32) * log_gamma[None, :]), 0.0)
        carry_term = jnp.einsum('rhd,hde->rhe', query_rows, prior_state, precision=lax.Precision.HIGHEST) * reach_decay[:, :, None]
        existing = lax.dynamic_slice_in_dim(carried, first_row, LMAX, 0)
        carried = lax.dynamic_update_slice_in_dim(carried, existing + carry_term, first_row, 0)
        tail_decay = jnp.where(in_turn[:, None], jnp.exp((turn_len - 1 - offsets)[:, None].astype(jnp.float32) * log_gamma[None, :]), 0.0)
        next_state = jnp.exp(turn_len.astype(jnp.float32) * log_gamma)[:, None, None] * prior_state + jnp.einsum('rhd,rhe->hde', key_rows * tail_decay[:, :, None], value_rows, precision=lax.Precision.HIGHEST)
        updated = lax.dynamic_update_index_in_dim(updated, next_state, pool_row, 0)
        return (carried, updated)
    carried, updated = lax.fori_loop(0, SESSIONS, visit_session, (jnp.zeros((row_total + LMAX, HEADS, VHEAD), jnp.float32), jnp.zeros_like(pool_states)))
    mixed = inside_sum + carried[:row_total]
    row_mean = lax.optimization_barrier(jnp.mean(mixed, axis=-1, keepdims=True))
    centered = mixed - row_mean
    variance = lax.optimization_barrier(jnp.mean(centered * centered, axis=-1, keepdims=True))
    normed = centered * lax.rsqrt(variance + norm_epsilon)
    gated = jax.nn.silu(gate.astype(jnp.float32)).reshape(row_total, HEADS, VHEAD) * normed
    retained = (gated * is_live[:, None, None].astype(jnp.float32)).astype(jnp.bfloat16).reshape(row_total, HEADS * VHEAD)
    return (retained, updated)
```

```python
import functools

import jax
import jax.numpy as jnp
from jax import lax
from jax.experimental import pallas as pl
from jax.experimental.pallas import tpu as pltpu
from jax.sharding import PartitionSpec as P

MESH = pl.DeviceIdType.MESH
HEAD = 256
ROWS = 512
SESSIONS = 32
OWNED = 8
SLOTS = 4
CHUNKS = 2
CHUNK = ROWS // CHUNKS
PER = CHUNK // 128
EPSILON = 1e-05
F32 = jnp.float32
BF16 = jnp.bfloat16


def kernel(
    tokens, w_query, w_key, w_value, w_gate, pool, decay, lengths, slot_of, serve,
    retained, keyval_out, *scratch,
):
    lines = [scratch[4 * r:4 * r + 4] for r in range(CHUNKS)]
    scratch = scratch[4 * CHUNKS:]
    twins = [scratch[4 * r:4 * r + 4] for r in range(CHUNKS)]
    scratch = scratch[4 * CHUNKS:]
    prior, packed, keyval, scratch = scratch[:4], scratch[4:7], scratch[7:11], scratch[11:]
    (
        weights, prior_own, query, gate, total, starts,
        token_sem, pool_sem, weight_sem, out_sem,
        near_send, near_recv, far_send, far_recv, twin_send, twin_recv,
        state_send, state_recv, kv_send, kv_recv, relay_send, relay_recv,
    ) = scratch
    me = lax.axis_index("pool")
    place = lax.axis_index("tp")
    x, z, core = place // 8, (place // 2) % 4, place % 2
    u = x * (1 - core) + z * core
    v = z * (1 - core) + x * core

    def at(u_at, v_at):
        u_at, v_at = (u_at + 4) % 4, (v_at + 4) % 4
        x_at = u_at * (1 - core) + v_at * core
        z_at = v_at * (1 - core) + u_at * core
        return {"tp": x_at * 8 + z_at * 2 + core}

    twin = {"tp": x * 8 + z * 2 + (1 - core)}

    def group(offset):
        return {"pool": (me + offset + 4) % 4}

    def remote(src, dst, send, recv, device):
        return pltpu.make_async_remote_copy(
            src_ref=src, dst_ref=dst, send_sem=send, recv_sem=recv,
            device_id=device, device_id_type=MESH,
        )

    def rows_of(r):
        return pl.ds(pl.multiple_of(r * CHUNK, CHUNK), CHUNK)

    token_copies = [
        pltpu.make_async_copy(
            tokens.at[pl.ds(r * CHUNK, CHUNK)], lines[r][0].at[0], token_sem.at[r]
        )
        for r in range(CHUNKS)
    ]
    for copy in token_copies:
        copy.start()
    pool_copy = pltpu.make_async_copy(pool, prior_own, pool_sem)
    pool_copy.start()
    matrices = (w_query, w_key, w_value, w_gate)

    def weight_copy(plane, line, which):
        source = matrices[which]
        part = source.at[:, line, 0] if plane == 0 else source.at[line, :, 1]
        return pltpu.make_async_copy(
            part, weights.at[plane, line, which], weight_sem.at[plane, line, which]
        )

    for line in range(4):
        for plane in range(2):
            for which in range(4):
                weight_copy(plane, line, which).start()

    partners = [at(u + d, v) for d in (1, 2, 3)] + [at(u, v + d) for d in (1, 2, 3)]
    partners += [twin] + [group(d) for d in (1, 2, 3)]
    barrier = pltpu.get_barrier_semaphore()
    for partner in partners:
        pl.semaphore_signal(barrier, inc=1, device_id=partner, device_id_type=MESH)
    pl.semaphore_wait(barrier, len(partners))

    def near(r, d):
        return remote(
            lines[r][0].at[0], lines[r][0].at[d],
            near_send.at[r, d - 1], near_recv.at[r, d - 1], at(u + d, v),
        )

    def far(r, d):
        return remote(
            lines[r][0], lines[r][d], far_send.at[r, d - 1], far_recv.at[r, d - 1], at(u, v + d)
        )

    def to_twin(r, d):
        return remote(lines[r][d], twins[r][d], twin_send.at[r, d], twin_recv.at[r, d], twin)

    for r in range(CHUNKS):
        token_copies[r].wait()
        for d in (1, 3, 2):
            near(r, d).start()

    zero = jnp.int32(0)

    def scan(s, carry):
        own_rows, own_count, ids, id_count, run = carry
        slot, to, long = slot_of[s], serve[s], lengths[s]
        owner, row = slot // OWNED, slot % OWNED
        begin = zero
        new_run = []
        for g in range(4):
            begin = jnp.where(to == g, run[g], begin)
            new_run.append(run[g] + jnp.where(to == g, long, 0))
        starts[s] = begin
        mine, here = owner == me, to == me
        ahead, behind = (to - me + 4) % 4, (me - owner + 4) % 4
        own_rows_n, own_count_n, ids_n, id_count_n = [], [], [], []
        for g in range(4):
            hit = mine & (ahead == g)
            own_rows_n.append(jnp.where(hit, own_rows[g] * 8 + row, own_rows[g]))
            own_count_n.append(own_count[g] + jnp.where(hit, 1, 0))
            hit = here & (behind == g)
            ids_n.append(jnp.where(hit, ids[g] * 32 + s, ids[g]))
            id_count_n.append(id_count[g] + jnp.where(hit, 1, 0))
        return (
            tuple(own_rows_n), tuple(own_count_n), tuple(ids_n), tuple(id_count_n),
            tuple(new_run),
        )

    four = (zero,) * 4
    own_rows, _, ids, id_count, _ = lax.fori_loop(
        0, SESSIONS, scan, (four, four, four, four, four)
    )

    def state(d, k):
        return remote(
            packed[d - 1].at[k], prior[d].at[k],
            state_send.at[d - 1, k], state_recv.at[d - 1, k], group(d),
        )

    pool_copy.wait()
    for k in range(SLOTS):
        for d in (2, 1, 3):
            packed[d - 1][k] = prior_own[(own_rows[d] >> (3 * k)) & 7].astype(BF16)
            state(d, k).start()
    for k in range(SLOTS):
        prior[0][k] = prior_own[(own_rows[0] >> (3 * k)) & 7].astype(BF16)

    def send_far(r):
        for d in (1, 2, 3):
            near(r, d).wait_recv()
        for d in (1, 3, 2):
            far(r, d).start()

    def multiply(part, plane, line, first):
        left = jnp.concatenate([part[i] for i in range(4)], axis=1)

        def one(which, _):
            right = jnp.concatenate(
                [weights[plane, line, which, (first - i + 4) % 4] for i in range(4)], axis=0
            )
            total[which] += jnp.dot(left, right, preferred_element_type=F32)
            return 0

        lax.fori_loop(0, 4, one, 0)

    def side(way):
        return group(1 if way == 0 else -1)

    def kv_out(r, way):
        return remote(
            keyval[0].at[r], keyval[1 + way].at[r], kv_send.at[r, way], kv_recv.at[r, way], side(way)
        )

    def relay(r, way):
        return remote(
            keyval[1 + way].at[r, way], keyval[3].at[r, way],
            relay_send.at[r, way], relay_recv.at[r, way], side(way),
        )

    send_far(0)
    for line in range(4):
        for plane in range(2):
            for which in range(4):
                weight_copy(plane, line, which).wait()

    for r in range(CHUNKS):
        total[...] = jnp.zeros_like(total)
        for j, d in enumerate((0, 1, 3, 2)):
            if j > 0:
                far(r, d).wait_recv()
            to_twin(r, d).start()
            if j == 2 and r + 1 < CHUNKS:
                send_far(r + 1)
            multiply(lines[r][d], core, (v - d + 4) % 4, u)
            to_twin(r, d).wait_recv()
            multiply(twins[r][d], 1 - core, (u - d + 4) % 4, v)
        query[r * CHUNK:(r + 1) * CHUNK, :] = total[0].astype(BF16)
        keyval[0][r, 0] = (total[1] * HEAD ** (-0.5)).astype(BF16)
        keyval[0][r, 1] = total[2].astype(BF16)
        gate[r * CHUNK:(r + 1) * CHUNK, :] = total[3].astype(BF16)
        kv_out(r, 0).start()
        kv_out(r, 1).start()

    def pass_on(r):
        for way in range(2):
            kv_out(r, way).wait_recv()
            relay(r, way).start()

    pass_on(0)

    for k in range(SLOTS):
        for d in (1, 2, 3):
            state(d, k).wait_recv()

    log_gamma = jnp.log(jnp.full((1, 1), decay[0], F32))

    first, last = [], []
    for g in range(4):
        for k in range(SLOTS):
            s = (ids[g] >> (5 * k)) & 31
            first.append(starts[s])
            last.append(jnp.where(k < id_count[g], starts[s] + lengths[s], 0))

    def own_rows_of(which):
        return jnp.concatenate([keyval[0][n, which] for n in range(CHUNKS)], axis=0)

    def retain(r, _):
        row = lax.broadcasted_iota(jnp.int32, (CHUNK, 1), 0) + r * CHUNK
        live = jnp.zeros((CHUNK, 1), jnp.bool_)
        begin = jnp.full((CHUNK, 1), ROWS, jnp.int32)
        q = query[rows_of(r), :]
        carried = jnp.zeros((CHUNK, HEAD), F32)
        for g in range(4):
            parts = []
            for k in range(SLOTS):
                n = g * SLOTS + k
                inside = (row >= first[n]) & (row < last[n])
                begin = jnp.where(inside, first[n], begin)
                parts.append(jnp.where(inside, q, jnp.zeros_like(q)))
            carried += jnp.dot(
                jnp.concatenate(parts, axis=1), prior[g][...].reshape(SLOTS * HEAD, HEAD),
                preferred_element_type=F32,
            )
        live = begin < ROWS
        column = lax.broadcasted_iota(jnp.int32, (CHUNK, ROWS), 1)
        distance = row - column
        scores = lax.dot_general(
            q, own_rows_of(0), (((1,), (1,)), ((), ())), preferred_element_type=F32
        )
        weight = jnp.exp(jnp.maximum(distance, 0).astype(F32) * log_gamma)
        mixing = jnp.where((distance >= 0) & (column >= begin), scores * weight, 0.0).astype(BF16)
        mixed = jnp.dot(
            mixing, own_rows_of(1), preferred_element_type=F32
        )
        reach = jnp.exp(jnp.maximum(row - begin + 1, 0).astype(F32) * log_gamma)
        mixed = mixed + carried * jnp.where(live, reach, 0.0)
        centered = mixed - jnp.mean(mixed, axis=-1, keepdims=True)
        variance = jnp.mean(centered * centered, axis=-1, keepdims=True)
        normed = centered * lax.rsqrt(variance + EPSILON)
        out = gate[rows_of(r), :].astype(F32)
        out = out * (1.0 / (1.0 + jnp.exp(-out))) * normed
        retained[rows_of(r), :] = jnp.where(live, out, 0.0).astype(BF16)
        return 0

    lax.fori_loop(0, CHUNKS, retain, 0)
    for r in range(1, CHUNKS):
        pass_on(r)
    for r in range(CHUNKS):
        for way in range(2):
            relay(r, way).wait_recv()
    out_copies = [
        pltpu.make_async_copy(keyval[n], keyval_out.at[n], out_sem.at[n]) for n in range(4)
    ]
    for copy in out_copies:
        copy.start()
    for r in range(CHUNKS):
        for d in (1, 2, 3):
            near(r, d).wait_send()
            far(r, d).wait_send()
        for d in range(4):
            to_twin(r, d).wait_send()
        for way in range(2):
            kv_out(r, way).wait_send()
            relay(r, way).wait_send()
    for k in range(SLOTS):
        for d in (1, 2, 3):
            state(d, k).wait_send()
    for copy in out_copies:
        copy.wait()


def update(keyval, pool, decay, lengths, slot_of, serve, new_states, starts):
    me = lax.axis_index("pool")
    zero = jnp.int32(0)

    def scan(s, run):
        to = serve[s]
        begin = zero
        for g in range(4):
            begin = jnp.where(to == g, run[g], begin)
        slot = slot_of[s]

        @pl.when(slot // OWNED == me)
        def _():
            away = (me - to + 4) % 4
            starts[0, slot % OWNED] = jnp.where(away == 3, 2, jnp.where(away == 2, 3, away))
            starts[1, slot % OWNED] = begin
            starts[2, slot % OWNED] = lengths[s]

        return tuple(run[g] + jnp.where(to == g, lengths[s], 0) for g in range(4))

    lax.fori_loop(0, SESSIONS, scan, (zero,) * 4)
    log_gamma = jnp.log(jnp.full((1, 1), decay[0], F32))

    def one(i, _):
        place, begin, long = starts[0, i], starts[1, i], starts[2, i]
        low = jnp.minimum(begin // 128, ROWS // 128 - 2)
        row = lax.broadcasted_iota(jnp.int32, (256, 1), 0) + low * 128

        def rows_at(which):
            return jnp.concatenate(
                [
                    keyval[
                        place, (low + n) // PER, which,
                        pl.ds(pl.multiple_of((low + n) % PER * 128, 128), 128), :,
                    ]
                    for n in range(2)
                ],
                axis=0,
            )

        behind = begin + long - 1 - row
        tail = jnp.exp(jnp.maximum(behind, 0).astype(F32) * log_gamma)
        tail = jnp.where((row >= begin) & (behind >= 0), tail, 0.0)
        k_rows = rows_at(0).astype(F32) * tail
        v_rows = rows_at(1)
        change = lax.dot_general(
            k_rows.astype(BF16), v_rows, (((0,), (0,)), ((), ())), preferred_element_type=F32
        )
        keep = jnp.exp(jnp.full((1, 1), long, jnp.int32).astype(F32) * log_gamma)
        new_states[i] = keep * pool[i] + change
        return 0

    lax.fori_loop(0, OWNED, one, 0, unroll=2)


def on_device(tokens, w_query, w_key, w_value, w_gate, decay, pool_states, lengths, slot_of, serve):
    hbm = pl.BlockSpec(memory_space=pl.ANY)
    vmem = pl.BlockSpec(memory_space=pltpu.VMEM)
    smem = pl.BlockSpec(memory_space=pltpu.SMEM)
    dma = pltpu.SemaphoreType.DMA
    split = [w.reshape(4, 4, 2, HEAD, HEAD) for w in (w_query, w_key, w_value, w_gate)]
    states = pool_states.reshape(OWNED, HEAD, HEAD)
    retained, keyval = pl.pallas_call(
        kernel,
        out_shape=(
            jax.ShapeDtypeStruct((ROWS, HEAD), BF16),
            jax.ShapeDtypeStruct((4, CHUNKS, 2, CHUNK, HEAD), BF16),
        ),
        in_specs=[hbm] * 6 + [smem] * 4,
        out_specs=(vmem, hbm),
        scratch_shapes=[
            *[pltpu.VMEM((4, CHUNK, HEAD), BF16)] * (8 * CHUNKS),
            *[pltpu.VMEM((SLOTS, HEAD, HEAD), BF16)] * 7,
            *[pltpu.VMEM((CHUNKS, 2, CHUNK, HEAD), BF16)] * 4,
            pltpu.VMEM((2, 4, 4, 4, HEAD, HEAD), BF16),
            pltpu.VMEM((OWNED, HEAD, HEAD), F32),
            pltpu.VMEM((ROWS, HEAD), BF16),
            pltpu.VMEM((ROWS, HEAD), BF16),
            pltpu.VMEM((4, CHUNK, HEAD), F32),
            pltpu.SMEM((SESSIONS,), jnp.int32),
            dma((CHUNKS,)), dma, dma((2, 4, 4)), dma((4,)),
            dma((CHUNKS, 3)), dma((CHUNKS, 3)),
            dma((CHUNKS, 3)), dma((CHUNKS, 3)),
            dma((CHUNKS, 4)), dma((CHUNKS, 4)),
            dma((3, SLOTS)), dma((3, SLOTS)),
            dma((CHUNKS, 2)), dma((CHUNKS, 2)),
            dma((CHUNKS, 2)), dma((CHUNKS, 2)),
        ],
        compiler_params=pltpu.CompilerParams(
            collective_id=0, has_side_effects=True, vmem_limit_bytes=56 << 20
        ),
        cost_estimate=pl.CostEstimate(
            flops=11_000_000_000, bytes_accessed=24_000_000, transcendentals=1_000_000
        ),
    )(tokens, *split, states, decay, lengths, slot_of, serve)
    new_states = pl.pallas_call(
        update,
        out_shape=jax.ShapeDtypeStruct((OWNED, HEAD, HEAD), F32),
        in_specs=[vmem, vmem] + [smem] * 4,
        out_specs=vmem,
        scratch_shapes=[pltpu.SMEM((3, OWNED), jnp.int32)],
        compiler_params=pltpu.CompilerParams(vmem_limit_bytes=24 << 20),
        cost_estimate=pl.CostEstimate(
            flops=300_000_000, bytes_accessed=6_000_000, transcendentals=2048
        ),
    )(keyval, states, decay, lengths, slot_of, serve)
    return retained, new_states.reshape(OWNED, 1, HEAD, HEAD)


def solution(mesh):
    return jax.shard_map(
        on_device,
        mesh=mesh,
        in_specs=(
            P("pool", "tp"),
            P(None, "tp"),
            P(None, "tp"),
            P(None, "tp"),
            P(None, "tp"),
            P("tp"),
            P("pool", "tp", None, None),
            P(),
            P(),
            P(),
        ),
        out_specs=(P("pool", "tp"), P("pool", "tp", None, None)),
        check_vma=False,
    )
```

```python
import functools

import jax
import jax.numpy as jnp
from jax import lax
from jax.experimental import pallas as pl
from jax.experimental.pallas import tpu as pltpu
from jax.sharding import PartitionSpec as P

MESH = pl.DeviceIdType.MESH
HEAD = 256
ROWS = 512
SESSIONS = 32
OWNED = 8
SLOTS = 4
CHUNKS = 2
CHUNK = ROWS // CHUNKS
PER = CHUNK // 128
STAGGER = 4.5
EPSILON = 1e-05
F32 = jnp.float32
BF16 = jnp.bfloat16


def kernel(
    tokens, w_query, w_key, w_value, w_gate, pool, decay, lengths, slot_of, serve,
    retained, keyval_out, *scratch,
):
    lines = [scratch[4 * r:4 * r + 4] for r in range(CHUNKS)]
    scratch = scratch[4 * CHUNKS:]
    twins = [scratch[4 * r:4 * r + 4] for r in range(CHUNKS)]
    scratch = scratch[4 * CHUNKS:]
    prior, packed, keyval, scratch = scratch[:4], scratch[4:7], scratch[7:11], scratch[11:]
    (
        weights, prior_own, query, gate, total, starts,
        token_sem, pool_sem, weight_sem, out_sem,
        near_send, near_recv, near2_send, near2_recv, far_send, far_recv, far2_send, far2_recv,
        twin_send, twin_recv, state_send, state_recv, kv_send, kv_recv, relay_send, relay_recv,
    ) = scratch
    me = lax.axis_index("pool")
    place = lax.axis_index("tp")
    x, z, core = place // 8, (place // 2) % 4, place % 2
    u = x * (1 - core) + z * core
    v = z * (1 - core) + x * core

    def at(u_at, v_at):
        u_at, v_at = (u_at + 4) % 4, (v_at + 4) % 4
        x_at = u_at * (1 - core) + v_at * core
        z_at = v_at * (1 - core) + u_at * core
        return {"tp": x_at * 8 + z_at * 2 + core}

    twin = {"tp": x * 8 + z * 2 + (1 - core)}

    def group(offset):
        return {"pool": (me + offset + 4) % 4}

    def remote(src, dst, send, recv, device):
        return pltpu.make_async_remote_copy(
            src_ref=src, dst_ref=dst, send_sem=send, recv_sem=recv,
            device_id=device, device_id_type=MESH,
        )

    def rows_of(r):
        return pl.ds(pl.multiple_of(r * CHUNK, CHUNK), CHUNK)

    token_copies = [
        pltpu.make_async_copy(
            tokens.at[pl.ds(r * CHUNK, CHUNK)], lines[r][0].at[0], token_sem.at[r]
        )
        for r in range(CHUNKS)
    ]
    for copy in token_copies:
        copy.start()
    pool_copy = pltpu.make_async_copy(pool, prior_own, pool_sem)
    pool_copy.start()
    matrices = (w_query, w_key, w_value, w_gate)

    def weight_copy(plane, line, which):
        source = matrices[which]
        part = source.at[:, line, 0] if plane == 0 else source.at[line, :, 1]
        return pltpu.make_async_copy(
            part, weights.at[plane, line, which], weight_sem.at[plane, line, which]
        )

    for line in range(4):
        for plane in range(2):
            for which in range(4):
                weight_copy(plane, line, which).start()

    partners = [at(u + 1, v), at(u - 1, v), at(u, v + 1), at(u, v - 1)]
    partners += [twin] + [group(d) for d in (1, 2, 3)]
    barrier = pltpu.get_barrier_semaphore()
    for partner in partners:
        pl.semaphore_signal(barrier, inc=1, device_id=partner, device_id_type=MESH)
    pl.semaphore_wait(barrier, len(partners))

    halves = (pl.ds(0, CHUNK // 2), pl.ds(CHUNK // 2, CHUNK // 2))

    def near(r, way):
        return remote(
            lines[r][0].at[0], lines[r][0].at[1 + 2 * way],
            near_send.at[r, way], near_recv.at[r, way], at(u + 1 - 2 * way, v),
        )

    def near2(r, way):
        return remote(
            lines[r][0].at[1 + 2 * way, halves[way]], lines[r][0].at[2, halves[way]],
            near2_send.at[r, way], near2_recv.at[r, way], at(u + 1 - 2 * way, v),
        )

    def far(r, i, way):
        return remote(
            lines[r][0].at[i], lines[r][1 + 2 * way].at[i],
            far_send.at[r, i, way], far_recv.at[r, i, way], at(u, v + 1 - 2 * way),
        )

    def far2(r, i, way):
        return remote(
            lines[r][1 + 2 * way].at[i, halves[way]], lines[r][2].at[i, halves[way]],
            far2_send.at[r, i, way], far2_recv.at[r, i, way], at(u, v + 1 - 2 * way),
        )

    def to_twin(r, d, i):
        return remote(
            lines[r][d].at[i], twins[r][d].at[i], twin_send.at[r, d, i], twin_recv.at[r, d, i], twin
        )

    def spread(r, i):
        for way in range(2):
            far(r, i, way).start()
        to_twin(r, 0, i).start()

    def open_chunk(r):
        token_copies[r].wait()
        for way in range(2):
            near(r, way).start()
        spread(r, 0)

    def near_in(r):
        for way in range(2):
            near(r, way).wait_recv()
            near2(r, way).start()
            spread(r, 1 + 2 * way)

    def near2_in(r):
        for way in range(2):
            near2(r, way).wait_recv()
        spread(r, 2)

    def far_in(r, i):
        for way in range(2):
            far(r, i, way).wait_recv()
            far2(r, i, way).start()
            to_twin(r, 1 + 2 * way, i).start()

    def far2_in(r, i):
        for way in range(2):
            far2(r, i, way).wait_recv()
        to_twin(r, 2, i).start()

    for r in range(CHUNKS):
        open_chunk(r)

    zero = jnp.int32(0)

    def scan(s, carry):
        own_rows, own_count, ids, id_count, run = carry
        slot, to, long = slot_of[s], serve[s], lengths[s]
        owner, row = slot // OWNED, slot % OWNED
        begin = zero
        new_run = []
        for g in range(4):
            begin = jnp.where(to == g, run[g], begin)
            new_run.append(run[g] + jnp.where(to == g, long, 0))
        starts[s] = begin
        mine, here = owner == me, to == me
        ahead, behind = (to - me + 4) % 4, (me - owner + 4) % 4
        own_rows_n, own_count_n, ids_n, id_count_n = [], [], [], []
        for g in range(4):
            hit = mine & (ahead == g)
            own_rows_n.append(jnp.where(hit, own_rows[g] * 8 + row, own_rows[g]))
            own_count_n.append(own_count[g] + jnp.where(hit, 1, 0))
            hit = here & (behind == g)
            ids_n.append(jnp.where(hit, ids[g] * 32 + s, ids[g]))
            id_count_n.append(id_count[g] + jnp.where(hit, 1, 0))
        return (
            tuple(own_rows_n), tuple(own_count_n), tuple(ids_n), tuple(id_count_n),
            tuple(new_run),
        )

    four = (zero,) * 4
    own_rows, _, ids, id_count, _ = lax.fori_loop(
        0, SESSIONS, scan, (four, four, four, four, four)
    )

    def state(d, k):
        return remote(
            packed[d - 1].at[k], prior[d].at[k],
            state_send.at[d - 1, k], state_recv.at[d - 1, k], group(d),
        )

    pool_copy.wait()
    for k in range(SLOTS):
        for d in (2, 1, 3):
            packed[d - 1][k] = prior_own[(own_rows[d] >> (3 * k)) & 7].astype(BF16)
            state(d, k).start()
    for k in range(SLOTS):
        prior[0][k] = prior_own[(own_rows[0] >> (3 * k)) & 7].astype(BF16)

    def multiply(part, plane, line, first, r, pair):
        left = jnp.concatenate([part[i] for i in range(4)], axis=1)

        def one(n, _):
            which = 1 + n if pair == 0 else 3 * n
            right = jnp.concatenate(
                [weights[plane, line, which, (first - i + 4) % 4] for i in range(4)], axis=0
            )
            total[r, n] += jnp.dot(left, right, preferred_element_type=F32)
            return 0

        lax.fori_loop(0, 2, one, 0, unroll=True)

    def own(r, d, pair=0):
        multiply(lines[r][d], core, (v - d + 4) % 4, u, r, pair)

    def other(r, d, pair=0):
        if pair == 0:
            for i in range(4):
                to_twin(r, d, i).wait_recv()
        multiply(twins[r][d], 1 - core, (u - d + 4) % 4, v, r, pair)

    def side(way):
        return group(1 if way == 0 else -1)

    def kv_out(r, way, which):
        return remote(
            keyval[0].at[r, which], keyval[1 + way].at[r, which],
            kv_send.at[r, way, which], kv_recv.at[r, way, which], side(way),
        )

    def relay(r, way):
        return remote(
            keyval[1 + way].at[r, way], keyval[3].at[r, way],
            relay_send.at[r, way], relay_recv.at[r, way], side(way),
        )

    def finish(r):
        keyval[0][r, 0] = (total[r, 0] * HEAD ** (-0.5)).astype(BF16)
        kv_out(r, 0, 0).start()
        keyval[0][r, 1] = total[r, 1].astype(BF16)
        kv_out(r, 1, 1).start()
        kv_out(r, 0, 1).start()
        kv_out(r, 1, 0).start()

    def pass_on(r):
        for way in range(2):
            kv_out(r, way, way).wait_recv()
            relay(r, way).start()

    def rest(r):
        total[r] = jnp.zeros_like(total[r])
        for d in range(4):
            own(r, d, 1)
            other(r, d, 1)
        query[r * CHUNK:(r + 1) * CHUNK, :] = total[r, 0].astype(BF16)
        gate[r * CHUNK:(r + 1) * CHUNK, :] = total[r, 1].astype(BF16)

    def get_weights(_):
        for line in range(4):
            for plane in range(2):
                for which in range(4):
                    weight_copy(plane, line, which).wait()

    steps = [
        (1, near_in), (2, far_in, 0), (3, near2_in), (4, far_in, 1), (5, far_in, 3), (6, far_in, 2),
        (7, far2_in, 0), (8, far2_in, 1), (9, far2_in, 3), (10, far2_in, 2),
        (6.5, own, 0), (7.5, other, 0), (8.2, own, 1), (8.7, own, 3), (9.5, other, 1),
        (9.7, other, 3), (10.5, own, 2), (11, other, 2), (11.5, finish),
    ]
    total[...] = jnp.zeros_like(total)
    order = [(when + STAGGER * r, r, *step) for r in range(CHUNKS) for when, *step in steps]
    order.append((6.4, 0, get_weights))
    for _, r, step, *more in sorted(order, key=lambda entry: entry[:2]):
        if step is finish and r > 0:
            pass_on(r - 1)
        step(r, *more)
    rest(0)
    pass_on(CHUNKS - 1)
    for r in range(1, CHUNKS):
        rest(r)

    for k in range(SLOTS):
        for d in (1, 2, 3):
            state(d, k).wait_recv()

    log_gamma = jnp.log(jnp.full((1, 1), decay[0], F32))

    first, last = [], []
    for g in range(4):
        for k in range(SLOTS):
            s = (ids[g] >> (5 * k)) & 31
            first.append(starts[s])
            last.append(jnp.where(k < id_count[g], starts[s] + lengths[s], 0))

    def own_rows_of(which):
        return jnp.concatenate([keyval[0][n, which] for n in range(CHUNKS)], axis=0)

    def retain(r, _):
        row = lax.broadcasted_iota(jnp.int32, (CHUNK, 1), 0) + r * CHUNK
        live = jnp.zeros((CHUNK, 1), jnp.bool_)
        begin = jnp.full((CHUNK, 1), ROWS, jnp.int32)
        q = query[rows_of(r), :]
        carried = jnp.zeros((CHUNK, HEAD), F32)
        for g in range(4):
            parts = []
            for k in range(SLOTS):
                n = g * SLOTS + k
                inside = (row >= first[n]) & (row < last[n])
                begin = jnp.where(inside, first[n], begin)
                parts.append(jnp.where(inside, q, jnp.zeros_like(q)))
            carried += jnp.dot(
                jnp.concatenate(parts, axis=1), prior[g][...].reshape(SLOTS * HEAD, HEAD),
                preferred_element_type=F32,
            )
        live = begin < ROWS
        column = lax.broadcasted_iota(jnp.int32, (CHUNK, ROWS), 1)
        distance = row - column
        scores = lax.dot_general(
            q, own_rows_of(0), (((1,), (1,)), ((), ())), preferred_element_type=F32
        )
        weight = jnp.exp(jnp.maximum(distance, 0).astype(F32) * log_gamma)
        mixing = jnp.where((distance >= 0) & (column >= begin), scores * weight, 0.0).astype(BF16)
        mixed = jnp.dot(
            mixing, own_rows_of(1), preferred_element_type=F32
        )
        reach = jnp.exp(jnp.maximum(row - begin + 1, 0).astype(F32) * log_gamma)
        mixed = mixed + carried * jnp.where(live, reach, 0.0)
        centered = mixed - jnp.mean(mixed, axis=-1, keepdims=True)
        variance = jnp.mean(centered * centered, axis=-1, keepdims=True)
        normed = centered * lax.rsqrt(variance + EPSILON)
        out = gate[rows_of(r), :].astype(F32)
        out = out * (1.0 / (1.0 + jnp.exp(-out))) * normed
        retained[rows_of(r), :] = jnp.where(live, out, 0.0).astype(BF16)
        return 0

    lax.fori_loop(0, CHUNKS, retain, 0)
    for r in range(CHUNKS):
        for way in range(2):
            kv_out(r, way, 1 - way).wait_recv()
    for r in range(CHUNKS):
        for way in range(2):
            relay(r, way).wait_recv()
    out_copies = [
        pltpu.make_async_copy(keyval[n], keyval_out.at[n], out_sem.at[n]) for n in range(4)
    ]
    for copy in out_copies:
        copy.start()
    for r in range(CHUNKS):
        for i in range(4):
            for d in range(4):
                to_twin(r, d, i).wait_send()
            for way in range(2):
                far(r, i, way).wait_send()
                far2(r, i, way).wait_send()
        for way in range(2):
            near(r, way).wait_send()
            near2(r, way).wait_send()
            for which in range(2):
                kv_out(r, way, which).wait_send()
            relay(r, way).wait_send()
    for k in range(SLOTS):
        for d in (1, 2, 3):
            state(d, k).wait_send()
    for copy in out_copies:
        copy.wait()


def update(keyval, pool, decay, lengths, slot_of, serve, new_states, starts):
    me = lax.axis_index("pool")
    zero = jnp.int32(0)

    def scan(s, run):
        to = serve[s]
        begin = zero
        for g in range(4):
            begin = jnp.where(to == g, run[g], begin)
        slot = slot_of[s]

        @pl.when(slot // OWNED == me)
        def _():
            away = (me - to + 4) % 4
            starts[0, slot % OWNED] = jnp.where(away == 3, 2, jnp.where(away == 2, 3, away))
            starts[1, slot % OWNED] = begin
            starts[2, slot % OWNED] = lengths[s]

        return tuple(run[g] + jnp.where(to == g, lengths[s], 0) for g in range(4))

    lax.fori_loop(0, SESSIONS, scan, (zero,) * 4)
    log_gamma = jnp.log(jnp.full((1, 1), decay[0], F32))

    def one(i, _):
        place, begin, long = starts[0, i], starts[1, i], starts[2, i]
        low = jnp.minimum(begin // 128, ROWS // 128 - 2)
        row = lax.broadcasted_iota(jnp.int32, (256, 1), 0) + low * 128

        def rows_at(which):
            return jnp.concatenate(
                [
                    keyval[
                        place, (low + n) // PER, which,
                        pl.ds(pl.multiple_of((low + n) % PER * 128, 128), 128), :,
                    ]
                    for n in range(2)
                ],
                axis=0,
            )

        behind = begin + long - 1 - row
        tail = jnp.exp(jnp.maximum(behind, 0).astype(F32) * log_gamma)
        tail = jnp.where((row >= begin) & (behind >= 0), tail, 0.0)
        k_rows = rows_at(0).astype(F32) * tail
        v_rows = rows_at(1)
        change = lax.dot_general(
            k_rows.astype(BF16), v_rows, (((0,), (0,)), ((), ())), preferred_element_type=F32
        )
        keep = jnp.exp(jnp.full((1, 1), long, jnp.int32).astype(F32) * log_gamma)
        new_states[i] = keep * pool[i] + change
        return 0

    lax.fori_loop(0, OWNED, one, 0, unroll=2)


def on_device(tokens, w_query, w_key, w_value, w_gate, decay, pool_states, lengths, slot_of, serve):
    hbm = pl.BlockSpec(memory_space=pl.ANY)
    vmem = pl.BlockSpec(memory_space=pltpu.VMEM)
    smem = pl.BlockSpec(memory_space=pltpu.SMEM)
    dma = pltpu.SemaphoreType.DMA
    split = [w.reshape(4, 4, 2, HEAD, HEAD) for w in (w_query, w_key, w_value, w_gate)]
    states = pool_states.reshape(OWNED, HEAD, HEAD)
    retained, keyval = pl.pallas_call(
        kernel,
        out_shape=(
            jax.ShapeDtypeStruct((ROWS, HEAD), BF16),
            jax.ShapeDtypeStruct((4, CHUNKS, 2, CHUNK, HEAD), BF16),
        ),
        in_specs=[hbm] * 6 + [smem] * 4,
        out_specs=(vmem, hbm),
        scratch_shapes=[
            *[pltpu.VMEM((4, CHUNK, HEAD), BF16)] * (8 * CHUNKS),
            *[pltpu.VMEM((SLOTS, HEAD, HEAD), BF16)] * 7,
            *[pltpu.VMEM((CHUNKS, 2, CHUNK, HEAD), BF16)] * 4,
            pltpu.VMEM((2, 4, 4, 4, HEAD, HEAD), BF16),
            pltpu.VMEM((OWNED, HEAD, HEAD), F32),
            pltpu.VMEM((ROWS, HEAD), BF16),
            pltpu.VMEM((ROWS, HEAD), BF16),
            pltpu.VMEM((CHUNKS, 2, CHUNK, HEAD), F32),
            pltpu.SMEM((SESSIONS,), jnp.int32),
            dma((CHUNKS,)), dma, dma((2, 4, 4)), dma((4,)),
            *[dma((CHUNKS, 2))] * 4,
            *[dma((CHUNKS, 4, 2))] * 4,
            *[dma((CHUNKS, 4, 4))] * 2,
            dma((3, SLOTS)), dma((3, SLOTS)),
            dma((CHUNKS, 2, 2)), dma((CHUNKS, 2, 2)),
            dma((CHUNKS, 2)), dma((CHUNKS, 2)),
        ],
        compiler_params=pltpu.CompilerParams(
            collective_id=0, has_side_effects=True, vmem_limit_bytes=56 << 20
        ),
        cost_estimate=pl.CostEstimate(
            flops=11_000_000_000, bytes_accessed=24_000_000, transcendentals=1_000_000
        ),
    )(tokens, *split, states, decay, lengths, slot_of, serve)
    new_states = pl.pallas_call(
        update,
        out_shape=jax.ShapeDtypeStruct((OWNED, HEAD, HEAD), F32),
        in_specs=[vmem, vmem] + [smem] * 4,
        out_specs=vmem,
        scratch_shapes=[pltpu.SMEM((3, OWNED), jnp.int32)],
        compiler_params=pltpu.CompilerParams(vmem_limit_bytes=24 << 20),
        cost_estimate=pl.CostEstimate(
            flops=300_000_000, bytes_accessed=6_000_000, transcendentals=2048
        ),
    )(keyval, states, decay, lengths, slot_of, serve)
    return retained, new_states.reshape(OWNED, 1, HEAD, HEAD)


def solution(mesh):
    return jax.shard_map(
        on_device,
        mesh=mesh,
        in_specs=(
            P("pool", "tp"),
            P(None, "tp"),
            P(None, "tp"),
            P(None, "tp"),
            P(None, "tp"),
            P("tp"),
            P("pool", "tp", None, None),
            P(),
            P(),
            P(),
        ),
        out_specs=(P("pool", "tp"), P("pool", "tp", None, None)),
        check_vma=False,
    )
```

```python
import functools

import jax
import jax.numpy as jnp
from jax import lax
from jax.experimental import pallas as pl
from jax.experimental.pallas import tpu as pltpu
from jax.sharding import PartitionSpec as P

MESH = pl.DeviceIdType.MESH
HEAD = 256
ROWS = 512
SESSIONS = 32
OWNED = 8
SLOTS = 4
LMAX = 128
SIZES = (256, 256)
CHUNKS = len(SIZES)
FIRST = tuple(sum(SIZES[:n]) for n in range(CHUNKS))
PART = 64
PARTS = ROWS // PART
SPAN = LMAX // PART + 1
BAND = 256
STAGGER = 4.5
EPSILON = 1e-05
F32 = jnp.float32
BF16 = jnp.bfloat16


def kernel(
    tokens, w_query, w_key, w_value, w_gate, pool, decay, lengths, slot_of, serve,
    retained, new_states, *scratch,
):
    lines = [scratch[4 * r:4 * r + 4] for r in range(CHUNKS)]
    scratch = scratch[4 * CHUNKS:]
    twins = [scratch[4 * r:4 * r + 4] for r in range(CHUNKS)]
    scratch = scratch[4 * CHUNKS:]
    prior, packed, keyval, scratch = scratch[:4], scratch[4:7], scratch[7:11], scratch[11:]
    total, scratch = scratch[:CHUNKS], scratch[CHUNKS:]
    (
        weights, prior_own, fresh, query, gate, starts,
        token_sem, pool_sem, weight_sem, out_sem,
        near_send, near_recv, near2_send, near2_recv, far_send, far_recv, far2_send, far2_recv,
        twin_send, twin_recv, state_send, state_recv, kv_send, kv_recv, relay_send, relay_recv,
    ) = scratch
    me = lax.axis_index("pool")
    place = lax.axis_index("tp")
    x, z, core = place // 8, (place // 2) % 4, place % 2
    u = x * (1 - core) + z * core
    v = z * (1 - core) + x * core

    def at(u_at, v_at):
        u_at, v_at = (u_at + 4) % 4, (v_at + 4) % 4
        x_at = u_at * (1 - core) + v_at * core
        z_at = v_at * (1 - core) + u_at * core
        return {"tp": x_at * 8 + z_at * 2 + core}

    twin = {"tp": x * 8 + z * 2 + (1 - core)}

    def group(offset):
        return {"pool": (me + offset + 4) % 4}

    def remote(src, dst, send, recv, device):
        return pltpu.make_async_remote_copy(
            src_ref=src, dst_ref=dst, send_sem=send, recv_sem=recv,
            device_id=device, device_id_type=MESH,
        )

    def rows_of(r):
        return pl.ds(FIRST[r], SIZES[r])

    token_copies = [
        pltpu.make_async_copy(
            tokens.at[rows_of(r)], lines[r][0].at[0], token_sem.at[r]
        )
        for r in range(CHUNKS)
    ]
    for copy in token_copies:
        copy.start()
    pool_copy = pltpu.make_async_copy(pool, prior_own, pool_sem)
    pool_copy.start()
    matrices = (w_query, w_key, w_value, w_gate)

    def weight_copy(plane, line, which):
        source = matrices[which]
        part = source.at[:, line, 0] if plane == 0 else source.at[line, :, 1]
        return pltpu.make_async_copy(
            part, weights.at[plane, line, which], weight_sem.at[plane, line, which]
        )

    for line in range(4):
        for plane in range(2):
            for which in range(4):
                weight_copy(plane, line, which).start()

    partners = [at(u + 1, v), at(u - 1, v), at(u + 2, v), at(u, v + 1), at(u, v - 1)]
    partners += [twin] + [group(d) for d in (1, 2, 3)]
    barrier = pltpu.get_barrier_semaphore()
    for partner in partners:
        pl.semaphore_signal(barrier, inc=1, device_id=partner, device_id_type=MESH)
    pl.semaphore_wait(barrier, len(partners))

    def half(r, way):
        return pl.ds(way * (SIZES[r] // 2), SIZES[r] // 2)

    def near(r, way):
        return remote(
            lines[r][0].at[0], lines[r][0].at[1 + 2 * way],
            near_send.at[r, way], near_recv.at[r, way], at(u + 1 - 2 * way, v),
        )

    def near2(r):
        return remote(
            lines[r][0].at[0], lines[r][0].at[2], near2_send.at[r], near2_recv.at[r], at(u + 2, v)
        )

    def far(r, i, way):
        return remote(
            lines[r][0].at[i], lines[r][1 + 2 * way].at[i],
            far_send.at[r, i, way], far_recv.at[r, i, way], at(u, v + 1 - 2 * way),
        )

    def far2(r, i, way):
        return remote(
            lines[r][1 + 2 * way].at[i, half(r, way)], lines[r][2].at[i, half(r, way)],
            far2_send.at[r, i, way], far2_recv.at[r, i, way], at(u, v + 1 - 2 * way),
        )

    def to_twin(r, d, i):
        return remote(
            lines[r][d].at[i], twins[r][d].at[i], twin_send.at[r, d, i], twin_recv.at[r, d, i], twin
        )

    def spread(r, i):
        for way in range(2):
            far(r, i, way).start()
        to_twin(r, 0, i).start()

    def open_chunk(r):
        token_copies[r].wait()
        for way in range(2):
            near(r, way).start()
        near2(r).start()
        spread(r, 0)

    def near_in(r):
        for way in range(2):
            near(r, way).wait_recv()
            spread(r, 1 + 2 * way)

    def near2_in(r):
        near2(r).wait_recv()
        spread(r, 2)

    def far_in(r, i):
        for way in range(2):
            far(r, i, way).wait_recv()
            far2(r, i, way).start()
            to_twin(r, 1 + 2 * way, i).start()

    def far2_in(r, i):
        for way in range(2):
            far2(r, i, way).wait_recv()
        to_twin(r, 2, i).start()

    for r in range(CHUNKS):
        open_chunk(r)

    zero = jnp.int32(0)

    def scan(s, carry):
        own_rows, own_count, ids, id_count, run, inverse = carry
        slot, to, long = slot_of[s], serve[s], lengths[s]
        owner, row = slot // OWNED, slot % OWNED
        begin = zero
        new_run = []
        for g in range(4):
            begin = jnp.where(to == g, run[g], begin)
            new_run.append(run[g] + jnp.where(to == g, long, 0))
        starts[s] = begin
        mine, here = owner == me, to == me
        ahead, behind = (to - me + 4) % 4, (me - owner + 4) % 4
        own_rows_n, own_count_n, ids_n, id_count_n = [], [], [], []
        for g in range(4):
            hit = mine & (ahead == g)
            own_rows_n.append(jnp.where(hit, own_rows[g] * 8 + row, own_rows[g]))
            own_count_n.append(own_count[g] + jnp.where(hit, 1, 0))
            hit = here & (behind == g)
            ids_n.append(jnp.where(hit, ids[g] * 32 + s, ids[g]))
            id_count_n.append(id_count[g] + jnp.where(hit, 1, 0))
        return (
            tuple(own_rows_n), tuple(own_count_n), tuple(ids_n), tuple(id_count_n),
            tuple(new_run),
            tuple(jnp.where(mine & (row == i), s, inverse[i]) for i in range(OWNED)),
        )

    four = (zero,) * 4
    own_rows, _, ids, id_count, _, inverse = lax.fori_loop(
        0, SESSIONS, scan, (four, four, four, four, four, (zero,) * OWNED)
    )

    def state(d, k):
        return remote(
            packed[d - 1].at[k], prior[d].at[k],
            state_send.at[d - 1, k], state_recv.at[d - 1, k], group(d),
        )

    pool_copy.wait()
    for k in range(SLOTS):
        for d in (2, 1, 3):
            packed[d - 1][k] = prior_own[(own_rows[d] >> (3 * k)) & 7].astype(BF16)
            state(d, k).start()
    for k in range(SLOTS):
        prior[0][k] = prior_own[(own_rows[0] >> (3 * k)) & 7].astype(BF16)

    def multiply(part, plane, line, first, r, pair):
        left = jnp.concatenate([part[i] for i in range(4)], axis=1)

        def one(n, _):
            which = 1 + n if pair == 0 else 3 * n
            right = jnp.concatenate(
                [weights[plane, line, which, (first - i + 4) % 4] for i in range(4)], axis=0
            )
            total[r][n] += jnp.dot(left, right, preferred_element_type=F32)
            return 0

        lax.fori_loop(0, 2, one, 0, unroll=True)

    def own(r, d, pair=0):
        multiply(lines[r][d], core, (v - d + 4) % 4, u, r, pair)

    def other(r, d, pair=0):
        if pair == 0:
            for i in range(4):
                to_twin(r, d, i).wait_recv()
        multiply(twins[r][d], 1 - core, (u - d + 4) % 4, v, r, pair)

    def side(way):
        return group(1 if way == 0 else -1)

    def parts_of(r):
        return pl.ds(FIRST[r] // PART, SIZES[r] // PART)

    def kv_out(r, way, which):
        return remote(
            keyval[0].at[which, parts_of(r)], keyval[1 + way].at[which, parts_of(r)],
            kv_send.at[r, way, which], kv_recv.at[r, way, which], side(way),
        )

    def relay(r, way):
        return remote(
            keyval[1 + way].at[way, parts_of(r)], keyval[3].at[way, parts_of(r)],
            relay_send.at[r, way], relay_recv.at[r, way], side(way),
        )

    def finish(r):
        shape = (SIZES[r] // PART, PART, HEAD)
        keyval[0][0, parts_of(r)] = (total[r][0] * HEAD ** (-0.5)).astype(BF16).reshape(shape)
        kv_out(r, 0, 0).start()
        keyval[0][1, parts_of(r)] = total[r][1].astype(BF16).reshape(shape)
        kv_out(r, 1, 1).start()
        kv_out(r, 0, 1).start()
        kv_out(r, 1, 0).start()

    def pass_on(r):
        for way in range(2):
            kv_out(r, way, way).wait_recv()
            relay(r, way).start()

    def rest(r):
        total[r][...] = jnp.zeros_like(total[r])
        for d in range(4):
            own(r, d, 1)
            other(r, d, 1)
        query[rows_of(r), :] = total[r][0].astype(BF16)
        gate[rows_of(r), :] = total[r][1].astype(BF16)

    def get_weights(_):
        for line in range(4):
            for plane in range(2):
                for which in range(4):
                    weight_copy(plane, line, which).wait()

    steps = [
        (1, near_in), (2, far_in, 0), (3, near2_in), (4, far_in, 1), (5, far_in, 3), (6, far_in, 2),
        (7, far2_in, 0), (8, far2_in, 1), (9, far2_in, 3), (10, far2_in, 2),
        (6.5, own, 0), (7.5, other, 0), (8.2, own, 1), (8.7, own, 3), (9.5, other, 1),
        (9.7, other, 3), (10.5, own, 2), (11, other, 2), (11.5, finish),
    ]
    for r in range(CHUNKS):
        total[r][...] = jnp.zeros_like(total[r])
    order = [(when + STAGGER * r, r, *step) for r in range(CHUNKS) for when, *step in steps]
    order.append((6.4, 0, get_weights))
    for _, r, step, *more in sorted(order, key=lambda entry: entry[:2]):
        if step is finish and r > 0:
            pass_on(r - 1)
        step(r, *more)
    rest(0)
    pass_on(CHUNKS - 1)
    for r in range(1, CHUNKS):
        rest(r)

    for k in range(SLOTS):
        for d in (1, 2, 3):
            state(d, k).wait_recv()

    log_gamma = jnp.log(jnp.full((1, 1), decay[0], F32))

    first, last = [], []
    for g in range(4):
        for k in range(SLOTS):
            s = (ids[g] >> (5 * k)) & 31
            first.append(starts[s])
            last.append(jnp.where(k < id_count[g], starts[s] + lengths[s], 0))

    def own_rows_of(which):
        return keyval[0][which].reshape(ROWS, HEAD)

    def retain(r, _):
        rows = pl.ds(pl.multiple_of(r * BAND, BAND), BAND)
        row = lax.broadcasted_iota(jnp.int32, (BAND, 1), 0) + r * BAND
        begin = jnp.full((BAND, 1), ROWS, jnp.int32)
        q = query[rows, :]
        carried = jnp.zeros((BAND, HEAD), F32)
        for g in range(4):
            parts = []
            for k in range(SLOTS):
                n = g * SLOTS + k
                inside = (row >= first[n]) & (row < last[n])
                begin = jnp.where(inside, first[n], begin)
                parts.append(jnp.where(inside, q, jnp.zeros_like(q)))
            carried += jnp.dot(
                jnp.concatenate(parts, axis=1), prior[g][...].reshape(SLOTS * HEAD, HEAD),
                preferred_element_type=F32,
            )
        live = begin < ROWS
        column = lax.broadcasted_iota(jnp.int32, (BAND, ROWS), 1)
        distance = row - column
        scores = lax.dot_general(
            q, own_rows_of(0), (((1,), (1,)), ((), ())), preferred_element_type=F32
        )
        weight = jnp.exp(jnp.maximum(distance, 0).astype(F32) * log_gamma)
        mixing = jnp.where((distance >= 0) & (column >= begin), scores * weight, 0.0).astype(BF16)
        mixed = jnp.dot(
            mixing, own_rows_of(1), preferred_element_type=F32
        )
        reach = jnp.exp(jnp.maximum(row - begin + 1, 0).astype(F32) * log_gamma)
        mixed = mixed + carried * jnp.where(live, reach, 0.0)
        centered = mixed - jnp.mean(mixed, axis=-1, keepdims=True)
        variance = jnp.mean(centered * centered, axis=-1, keepdims=True)
        normed = centered * lax.rsqrt(variance + EPSILON)
        out = gate[rows, :].astype(F32)
        out = out * (1.0 / (1.0 + jnp.exp(-out))) * normed
        retained[rows, :] = jnp.where(live, out, 0.0).astype(BF16)
        return 0

    lax.fori_loop(0, ROWS // BAND, retain, 0)
    for r in range(CHUNKS):
        for way in range(2):
            kv_out(r, way, 1 - way).wait_recv()
    for r in range(CHUNKS):
        for way in range(2):
            relay(r, way).wait_recv()
    out_copies = []
    for i in range(OWNED):
        s = inverse[i]
        begin, long = starts[s], lengths[s]
        away = (me - serve[s] + 4) % 4
        low = jnp.minimum(begin // PART, PARTS - SPAN)
        row = lax.broadcasted_iota(jnp.int32, (SPAN * PART, 1), 0) + low * PART
        behind = begin + long - 1 - row
        tail = jnp.exp(jnp.maximum(behind, 0).astype(F32) * log_gamma)
        tail = jnp.where((row >= begin) & (behind >= 0), tail, 0.0)

        def turn_rows(which):
            blocks = []
            for n in range(SPAN):
                block = keyval[0][which, low + n]
                for place, group_away in ((1, 1), (2, 3), (3, 2)):
                    block = jnp.where(away == group_away, keyval[place][which, low + n], block)
                blocks.append(block)
            return jnp.concatenate(blocks, axis=0)

        change = lax.dot_general(
            (turn_rows(0).astype(F32) * tail).astype(BF16), turn_rows(1),
            (((0,), (0,)), ((), ())), preferred_element_type=F32,
        )
        keep = jnp.exp(jnp.full((1, 1), long, jnp.int32).astype(F32) * log_gamma)
        fresh[i] = keep * prior_own[i] + change
        out_copies.append(pltpu.make_async_copy(fresh.at[i], new_states.at[i], out_sem.at[i]))
        out_copies[i].start()
    for r in range(CHUNKS):
        for i in range(4):
            for d in range(4):
                to_twin(r, d, i).wait_send()
            for way in range(2):
                far(r, i, way).wait_send()
                far2(r, i, way).wait_send()
        near2(r).wait_send()
        for way in range(2):
            near(r, way).wait_send()
            for which in range(2):
                kv_out(r, way, which).wait_send()
            relay(r, way).wait_send()
    for k in range(SLOTS):
        for d in (1, 2, 3):
            state(d, k).wait_send()
    for copy in out_copies:
        copy.wait()


def deliver(retained, new_states, retained_out, new_states_out, rows, states, sem):
    passes = [(retained, rows, retained_out)]
    passes += [(new_states.at[i], states.at[i], new_states_out.at[i]) for i in range(OWNED)]
    loads = [
        pltpu.make_async_copy(src, held, sem.at[n, 0]) for n, (src, held, _) in enumerate(passes)
    ]
    stores = [
        pltpu.make_async_copy(held, dst, sem.at[n, 1]) for n, (_, held, dst) in enumerate(passes)
    ]
    for load in loads:
        load.start()
    for load, store in zip(loads, stores):
        load.wait()
        store.start()
    for store in stores:
        store.wait()


def on_device(tokens, w_query, w_key, w_value, w_gate, decay, pool_states, lengths, slot_of, serve):
    hbm = pl.BlockSpec(memory_space=pl.ANY)
    vmem = pl.BlockSpec(memory_space=pltpu.VMEM)
    smem = pl.BlockSpec(memory_space=pltpu.SMEM)
    dma = pltpu.SemaphoreType.DMA
    split = [w.reshape(4, 4, 2, HEAD, HEAD) for w in (w_query, w_key, w_value, w_gate)]
    states = pool_states.reshape(OWNED, HEAD, HEAD)
    retained, new_states = pl.pallas_call(
        kernel,
        out_shape=(
            jax.ShapeDtypeStruct((ROWS, HEAD), BF16),
            jax.ShapeDtypeStruct((OWNED, HEAD, HEAD), F32),
        ),
        in_specs=[hbm] * 6 + [smem] * 4,
        out_specs=(vmem, hbm),
        scratch_shapes=[
            *[pltpu.VMEM((4, size, HEAD), BF16) for size in SIZES for _ in range(4)] * 2,
            *[pltpu.VMEM((SLOTS, HEAD, HEAD), BF16)] * 7,
            *[pltpu.VMEM((2, PARTS, PART, HEAD), BF16)] * 4,
            *[pltpu.VMEM((2, size, HEAD), F32) for size in SIZES],
            pltpu.VMEM((2, 4, 4, 4, HEAD, HEAD), BF16),
            *[pltpu.VMEM((OWNED, HEAD, HEAD), F32)] * 2,
            pltpu.VMEM((ROWS, HEAD), BF16),
            pltpu.VMEM((ROWS, HEAD), BF16),
            pltpu.SMEM((SESSIONS,), jnp.int32),
            dma((CHUNKS,)), dma, dma((2, 4, 4)), dma((OWNED,)),
            *[dma((CHUNKS, 2))] * 2,
            *[dma((CHUNKS,))] * 2,
            *[dma((CHUNKS, 4, 2))] * 4,
            *[dma((CHUNKS, 4, 4))] * 2,
            dma((3, SLOTS)), dma((3, SLOTS)),
            dma((CHUNKS, 2, 2)), dma((CHUNKS, 2, 2)),
            dma((CHUNKS, 2)), dma((CHUNKS, 2)),
        ],
        compiler_params=pltpu.CompilerParams(
            collective_id=0, has_side_effects=True, vmem_limit_bytes=56 << 20
        ),
        cost_estimate=pl.CostEstimate(
            flops=11_000_000_000, bytes_accessed=24_000_000, transcendentals=1_000_000
        ),
    )(tokens, *split, states, decay, lengths, slot_of, serve)
    retained, new_states = pl.pallas_call(
        deliver,
        out_shape=(
            jax.ShapeDtypeStruct(retained.shape, BF16),
            jax.ShapeDtypeStruct(new_states.shape, F32),
        ),
        in_specs=[hbm, hbm],
        out_specs=(hbm, hbm),
        scratch_shapes=[
            pltpu.VMEM(retained.shape, BF16),
            pltpu.VMEM(new_states.shape, F32),
            dma((OWNED + 1, 2)),
        ],
    )(retained, new_states)
    return retained, new_states.reshape(OWNED, 1, HEAD, HEAD)


def solution(mesh):
    return jax.shard_map(
        on_device,
        mesh=mesh,
        in_specs=(
            P("pool", "tp"),
            P(None, "tp"),
            P(None, "tp"),
            P(None, "tp"),
            P(None, "tp"),
            P("tp"),
            P("pool", "tp", None, None),
            P(),
            P(),
            P(),
        ),
        out_specs=(P("pool", "tp"), P("pool", "tp", None, None)),
        check_vma=False,
    )
```

```python
import functools

import jax
import jax.numpy as jnp
from jax import lax
from jax.experimental import pallas as pl
from jax.experimental.pallas import tpu as pltpu
from jax.sharding import PartitionSpec as P

MESH = pl.DeviceIdType.MESH
HEAD = 256
ROWS = 512
SESSIONS = 32
OWNED = 8
SLOTS = 4
LMAX = 128
SIZES = (256, 256)
CHUNKS = len(SIZES)
FIRST = tuple(sum(SIZES[:n]) for n in range(CHUNKS))
PART = 64
PARTS = ROWS // PART
SPAN = LMAX // PART + 1
BAND = 256
STAGGER = 4.5
EPSILON = 1e-05
F32 = jnp.float32
BF16 = jnp.bfloat16


def kernel(
    tokens, w_query, w_key, w_value, w_gate, pool, decay, lengths, slot_of, serve,
    retained, new_states, *scratch,
):
    lines = [scratch[4 * r:4 * r + 4] for r in range(CHUNKS)]
    scratch = scratch[4 * CHUNKS:]
    twins = [scratch[4 * r:4 * r + 4] for r in range(CHUNKS)]
    scratch = scratch[4 * CHUNKS:]
    prior, packed, keyval, scratch = scratch[:4], scratch[4:7], scratch[7:11], scratch[11:]
    total, scratch = scratch[:CHUNKS], scratch[CHUNKS:]
    (
        weights, prior_own, fresh, query, gate, starts,
        token_sem, pool_sem, weight_sem, out_sem,
        near_send, near_recv, near2_send, near2_recv, far_send, far_recv, far2_send, far2_recv,
        twin_send, twin_recv, state_send, state_recv, kv_send, kv_recv, relay_send, relay_recv,
    ) = scratch
    me = lax.axis_index("pool")
    place = lax.axis_index("tp")
    x, z, core = place // 8, (place // 2) % 4, place % 2
    u = x * (1 - core) + z * core
    v = z * (1 - core) + x * core

    def at(u_at, v_at):
        u_at, v_at = (u_at + 4) % 4, (v_at + 4) % 4
        x_at = u_at * (1 - core) + v_at * core
        z_at = v_at * (1 - core) + u_at * core
        return {"tp": x_at * 8 + z_at * 2 + core}

    twin = {"tp": x * 8 + z * 2 + (1 - core)}

    def group(offset):
        return {"pool": (me + offset + 4) % 4}

    def remote(src, dst, send, recv, device):
        return pltpu.make_async_remote_copy(
            src_ref=src, dst_ref=dst, send_sem=send, recv_sem=recv,
            device_id=device, device_id_type=MESH,
        )

    def rows_of(r):
        return pl.ds(FIRST[r], SIZES[r])

    partners = [at(u + 1, v), at(u - 1, v), at(u + 2, v), at(u, v + 1), at(u, v - 1)]
    partners += [twin] + [group(d) for d in (1, 2, 3)]
    barrier = pltpu.get_barrier_semaphore()
    for partner in partners:
        pl.semaphore_signal(barrier, inc=1, device_id=partner, device_id_type=MESH)

    token_copies = [
        pltpu.make_async_copy(
            tokens.at[rows_of(r)], lines[r][0].at[0], token_sem.at[r]
        )
        for r in range(CHUNKS)
    ]
    for copy in token_copies:
        copy.start()
    pool_copy = pltpu.make_async_copy(pool, prior_own, pool_sem)
    pool_copy.start()
    matrices = (w_query, w_key, w_value, w_gate)

    def weight_copy(plane, line, which):
        source = matrices[which]
        part = source.at[:, line, 0] if plane == 0 else source.at[line, :, 1]
        return pltpu.make_async_copy(
            part, weights.at[plane, line, which], weight_sem.at[plane, line, which]
        )

    def half(r, way):
        return pl.ds(way * (SIZES[r] // 2), SIZES[r] // 2)

    def near(r, way):
        return remote(
            lines[r][0].at[0], lines[r][0].at[1 + 2 * way],
            near_send.at[r, way], near_recv.at[r, way], at(u + 1 - 2 * way, v),
        )

    def near2(r):
        return remote(
            lines[r][0].at[0], lines[r][0].at[2], near2_send.at[r], near2_recv.at[r], at(u + 2, v)
        )

    def far(r, i, way):
        return remote(
            lines[r][0].at[i], lines[r][1 + 2 * way].at[i],
            far_send.at[r, i, way], far_recv.at[r, i, way], at(u, v + 1 - 2 * way),
        )

    def far2(r, i, way):
        return remote(
            lines[r][1 + 2 * way].at[i, half(r, way)], lines[r][2].at[i, half(r, way)],
            far2_send.at[r, i, way], far2_recv.at[r, i, way], at(u, v + 1 - 2 * way),
        )

    def to_twin(r, d, i):
        return remote(
            lines[r][d].at[i], twins[r][d].at[i], twin_send.at[r, d, i], twin_recv.at[r, d, i], twin
        )

    def spread(r, i):
        for way in range(2):
            far(r, i, way).start()
        to_twin(r, 0, i).start()

    def open_chunk(r):
        token_copies[r].wait()
        for way in range(2):
            near(r, way).start()
        near2(r).start()
        spread(r, 0)

    def near_in(r):
        for way in range(2):
            near(r, way).wait_recv()
            spread(r, 1 + 2 * way)

    def near2_in(r):
        near2(r).wait_recv()
        spread(r, 2)

    def far_in(r, i):
        for way in range(2):
            far(r, i, way).wait_recv()
            far2(r, i, way).start()
            to_twin(r, 1 + 2 * way, i).start()

    def far2_in(r, i):
        for way in range(2):
            far2(r, i, way).wait_recv()
        to_twin(r, 2, i).start()

    pl.semaphore_wait(barrier, len(partners))
    for r in range(CHUNKS):
        open_chunk(r)

    zero = jnp.int32(0)

    def scan(s, carry):
        own_rows, own_count, ids, id_count, run, inverse = carry
        slot, to, long = slot_of[s], serve[s], lengths[s]
        owner, row = slot // OWNED, slot % OWNED
        begin = zero
        new_run = []
        for g in range(4):
            begin = jnp.where(to == g, run[g], begin)
            new_run.append(run[g] + jnp.where(to == g, long, 0))
        starts[s] = begin
        mine, here = owner == me, to == me
        ahead, behind = (to - me + 4) % 4, (me - owner + 4) % 4
        own_rows_n, own_count_n, ids_n, id_count_n = [], [], [], []
        for g in range(4):
            hit = mine & (ahead == g)
            own_rows_n.append(jnp.where(hit, own_rows[g] * 8 + row, own_rows[g]))
            own_count_n.append(own_count[g] + jnp.where(hit, 1, 0))
            hit = here & (behind == g)
            ids_n.append(jnp.where(hit, ids[g] * 32 + s, ids[g]))
            id_count_n.append(id_count[g] + jnp.where(hit, 1, 0))
        return (
            tuple(own_rows_n), tuple(own_count_n), tuple(ids_n), tuple(id_count_n),
            tuple(new_run),
            tuple(jnp.where(mine & (row == i), s, inverse[i]) for i in range(OWNED)),
        )

    four = (zero,) * 4
    own_rows, _, ids, id_count, _, inverse = lax.fori_loop(
        0, SESSIONS, scan, (four, four, four, four, four, (zero,) * OWNED)
    )

    def state(d, k):
        return remote(
            packed[d - 1].at[k], prior[d].at[k],
            state_send.at[d - 1, k], state_recv.at[d - 1, k], group(d),
        )

    pool_copy.wait()
    for k in range(SLOTS):
        for d in (2, 1, 3):
            packed[d - 1][k] = prior_own[(own_rows[d] >> (3 * k)) & 7].astype(BF16)
            state(d, k).start()
    for k in range(SLOTS):
        prior[0][k] = prior_own[(own_rows[0] >> (3 * k)) & 7].astype(BF16)

    for line in range(4):
        for plane in range(2):
            for which in range(4):
                weight_copy(plane, line, which).start()

    def multiply(part, plane, line, first, r, pair):
        left = jnp.concatenate([part[i] for i in range(4)], axis=1)

        def one(n, _):
            which = 1 + n if pair == 0 else 3 * n
            right = jnp.concatenate(
                [weights[plane, line, which, (first - i + 4) % 4] for i in range(4)], axis=0
            )
            total[r][n] += jnp.dot(left, right, preferred_element_type=F32)
            return 0

        lax.fori_loop(0, 2, one, 0, unroll=True)

    def own(r, d, pair=0):
        multiply(lines[r][d], core, (v - d + 4) % 4, u, r, pair)

    def other(r, d, pair=0):
        if pair == 0:
            for i in range(4):
                to_twin(r, d, i).wait_recv()
        multiply(twins[r][d], 1 - core, (u - d + 4) % 4, v, r, pair)

    def side(way):
        return group(1 if way == 0 else -1)

    def parts_of(r):
        return pl.ds(FIRST[r] // PART, SIZES[r] // PART)

    def kv_out(r, way, which):
        return remote(
            keyval[0].at[which, parts_of(r)], keyval[1 + way].at[which, parts_of(r)],
            kv_send.at[r, way, which], kv_recv.at[r, way, which], side(way),
        )

    def relay(r, way):
        return remote(
            keyval[1 + way].at[way, parts_of(r)], keyval[3].at[way, parts_of(r)],
            relay_send.at[r, way], relay_recv.at[r, way], side(way),
        )

    def finish(r):
        shape = (SIZES[r] // PART, PART, HEAD)
        keyval[0][0, parts_of(r)] = (total[r][0] * HEAD ** (-0.5)).astype(BF16).reshape(shape)
        kv_out(r, 0, 0).start()
        keyval[0][1, parts_of(r)] = total[r][1].astype(BF16).reshape(shape)
        kv_out(r, 1, 1).start()
        kv_out(r, 0, 1).start()
        kv_out(r, 1, 0).start()

    def pass_on(r):
        for way in range(2):
            kv_out(r, way, way).wait_recv()
            relay(r, way).start()

    def rest(r):
        total[r][...] = jnp.zeros_like(total[r])
        for d in range(4):
            own(r, d, 1)
            other(r, d, 1)
        query[rows_of(r), :] = total[r][0].astype(BF16)
        gate[rows_of(r), :] = total[r][1].astype(BF16)

    def get_weights(_):
        for line in range(4):
            for plane in range(2):
                for which in range(4):
                    weight_copy(plane, line, which).wait()

    steps = [
        (1, near_in), (2, far_in, 0), (3, near2_in), (4, far_in, 1), (5, far_in, 3), (6, far_in, 2),
        (7, far2_in, 0), (8, far2_in, 1), (9, far2_in, 3), (10, far2_in, 2),
        (6.5, own, 0), (7.5, other, 0), (8.2, own, 1), (8.7, own, 3), (9.5, other, 1),
        (9.7, other, 3), (10.5, own, 2), (11, other, 2), (11.5, finish),
    ]
    for r in range(CHUNKS):
        total[r][...] = jnp.zeros_like(total[r])
    order = [(when + STAGGER * r, r, *step) for r in range(CHUNKS) for when, *step in steps]
    order.append((6.4, 0, get_weights))
    for _, r, step, *more in sorted(order, key=lambda entry: entry[:2]):
        if step is finish and r > 0:
            pass_on(r - 1)
        step(r, *more)
    rest(0)
    pass_on(CHUNKS - 1)
    for r in range(1, CHUNKS):
        rest(r)

    for k in range(SLOTS):
        for d in (1, 2, 3):
            state(d, k).wait_recv()

    log_gamma = jnp.log(jnp.full((1, 1), decay[0], F32))

    first, last = [], []
    for g in range(4):
        for k in range(SLOTS):
            s = (ids[g] >> (5 * k)) & 31
            first.append(starts[s])
            last.append(jnp.where(k < id_count[g], starts[s] + lengths[s], 0))

    def own_rows_of(which):
        return keyval[0][which].reshape(ROWS, HEAD)

    def retain(r, _):
        rows = pl.ds(pl.multiple_of(r * BAND, BAND), BAND)
        row = lax.broadcasted_iota(jnp.int32, (BAND, 1), 0) + r * BAND
        begin = jnp.full((BAND, 1), ROWS, jnp.int32)
        q = query[rows, :]
        carried = jnp.zeros((BAND, HEAD), F32)
        for g in range(4):
            parts = []
            for k in range(SLOTS):
                n = g * SLOTS + k
                inside = (row >= first[n]) & (row < last[n])
                begin = jnp.where(inside, first[n], begin)
                parts.append(jnp.where(inside, q, jnp.zeros_like(q)))
            carried += jnp.dot(
                jnp.concatenate(parts, axis=1), prior[g][...].reshape(SLOTS * HEAD, HEAD),
                preferred_element_type=F32,
            )
        live = begin < ROWS
        column = lax.broadcasted_iota(jnp.int32, (BAND, ROWS), 1)
        distance = row - column
        scores = lax.dot_general(
            q, own_rows_of(0), (((1,), (1,)), ((), ())), preferred_element_type=F32
        )
        weight = jnp.exp(jnp.maximum(distance, 0).astype(F32) * log_gamma)
        mixing = jnp.where((distance >= 0) & (column >= begin), scores * weight, 0.0).astype(BF16)
        mixed = jnp.dot(
            mixing, own_rows_of(1), preferred_element_type=F32
        )
        reach = jnp.exp(jnp.maximum(row - begin + 1, 0).astype(F32) * log_gamma)
        mixed = mixed + carried * jnp.where(live, reach, 0.0)
        centered = mixed - jnp.mean(mixed, axis=-1, keepdims=True)
        variance = jnp.mean(centered * centered, axis=-1, keepdims=True)
        normed = centered * lax.rsqrt(variance + EPSILON)
        out = gate[rows, :].astype(F32)
        out = out * (1.0 / (1.0 + jnp.exp(-out))) * normed
        retained[rows, :] = jnp.where(live, out, 0.0).astype(BF16)
        return 0

    lax.fori_loop(0, ROWS // BAND, retain, 0)
    for r in range(CHUNKS):
        for way in range(2):
            kv_out(r, way, 1 - way).wait_recv()
    for r in range(CHUNKS):
        for way in range(2):
            relay(r, way).wait_recv()
    out_copies = []
    for i in range(OWNED):
        s = inverse[i]
        begin, long = starts[s], lengths[s]
        away = (me - serve[s] + 4) % 4
        low = jnp.minimum(begin // PART, PARTS - SPAN)
        row = lax.broadcasted_iota(jnp.int32, (SPAN * PART, 1), 0) + low * PART
        behind = begin + long - 1 - row
        tail = jnp.exp(jnp.maximum(behind, 0).astype(F32) * log_gamma)
        tail = jnp.where((row >= begin) & (behind >= 0), tail, 0.0)

        def turn_rows(which):
            blocks = []
            for n in range(SPAN):
                block = keyval[0][which, low + n]
                for place, group_away in ((1, 1), (2, 3), (3, 2)):
                    block = jnp.where(away == group_away, keyval[place][which, low + n], block)
                blocks.append(block)
            return jnp.concatenate(blocks, axis=0)

        change = lax.dot_general(
            (turn_rows(0).astype(F32) * tail).astype(BF16), turn_rows(1),
            (((0,), (0,)), ((), ())), preferred_element_type=F32,
        )
        keep = jnp.exp(jnp.full((1, 1), long, jnp.int32).astype(F32) * log_gamma)
        fresh[i] = keep * prior_own[i] + change
        out_copies.append(pltpu.make_async_copy(fresh.at[i], new_states.at[i], out_sem.at[i]))
        out_copies[i].start()
    for r in range(CHUNKS):
        for i in range(4):
            for d in range(4):
                to_twin(r, d, i).wait_send()
            for way in range(2):
                far(r, i, way).wait_send()
                far2(r, i, way).wait_send()
        near2(r).wait_send()
        for way in range(2):
            near(r, way).wait_send()
            for which in range(2):
                kv_out(r, way, which).wait_send()
            relay(r, way).wait_send()
    for k in range(SLOTS):
        for d in (1, 2, 3):
            state(d, k).wait_send()
    for copy in out_copies:
        copy.wait()


def deliver(retained, new_states, retained_out, new_states_out, rows, states, sem):
    passes = [(retained, rows, retained_out)]
    passes += [(new_states.at[i], states.at[i], new_states_out.at[i]) for i in range(OWNED)]
    loads = [
        pltpu.make_async_copy(src, held, sem.at[n, 0]) for n, (src, held, _) in enumerate(passes)
    ]
    stores = [
        pltpu.make_async_copy(held, dst, sem.at[n, 1]) for n, (_, held, dst) in enumerate(passes)
    ]
    for load in loads:
        load.start()
    for load, store in zip(loads, stores):
        load.wait()
        store.start()
    for store in stores:
        store.wait()


def on_device(tokens, w_query, w_key, w_value, w_gate, decay, pool_states, lengths, slot_of, serve):
    hbm = pl.BlockSpec(memory_space=pl.ANY)
    vmem = pl.BlockSpec(memory_space=pltpu.VMEM)
    smem = pl.BlockSpec(memory_space=pltpu.SMEM)
    dma = pltpu.SemaphoreType.DMA
    split = [w.reshape(4, 4, 2, HEAD, HEAD) for w in (w_query, w_key, w_value, w_gate)]
    states = pool_states.reshape(OWNED, HEAD, HEAD)
    retained, new_states = pl.pallas_call(
        kernel,
        out_shape=(
            jax.ShapeDtypeStruct((ROWS, HEAD), BF16),
            jax.ShapeDtypeStruct((OWNED, HEAD, HEAD), F32),
        ),
        in_specs=[hbm] * 6 + [smem] * 4,
        out_specs=(vmem, hbm),
        scratch_shapes=[
            *[pltpu.VMEM((4, size, HEAD), BF16) for size in SIZES for _ in range(4)] * 2,
            *[pltpu.VMEM((SLOTS, HEAD, HEAD), BF16)] * 7,
            *[pltpu.VMEM((2, PARTS, PART, HEAD), BF16)] * 4,
            *[pltpu.VMEM((2, size, HEAD), F32) for size in SIZES],
            pltpu.VMEM((2, 4, 4, 4, HEAD, HEAD), BF16),
            *[pltpu.VMEM((OWNED, HEAD, HEAD), F32)] * 2,
            pltpu.VMEM((ROWS, HEAD), BF16),
            pltpu.VMEM((ROWS, HEAD), BF16),
            pltpu.SMEM((SESSIONS,), jnp.int32),
            dma((CHUNKS,)), dma, dma((2, 4, 4)), dma((OWNED,)),
            *[dma((CHUNKS, 2))] * 2,
            *[dma((CHUNKS,))] * 2,
            *[dma((CHUNKS, 4, 2))] * 4,
            *[dma((CHUNKS, 4, 4))] * 2,
            dma((3, SLOTS)), dma((3, SLOTS)),
            dma((CHUNKS, 2, 2)), dma((CHUNKS, 2, 2)),
            dma((CHUNKS, 2)), dma((CHUNKS, 2)),
        ],
        compiler_params=pltpu.CompilerParams(
            collective_id=0, has_side_effects=True, vmem_limit_bytes=56 << 20
        ),
        cost_estimate=pl.CostEstimate(
            flops=11_000_000_000, bytes_accessed=24_000_000, transcendentals=1_000_000
        ),
    )(tokens, *split, states, decay, lengths, slot_of, serve)
    retained, new_states = pl.pallas_call(
        deliver,
        out_shape=(
            jax.ShapeDtypeStruct(retained.shape, BF16),
            jax.ShapeDtypeStruct(new_states.shape, F32),
        ),
        in_specs=[hbm, hbm],
        out_specs=(hbm, hbm),
        scratch_shapes=[
            pltpu.VMEM(retained.shape, BF16),
            pltpu.VMEM(new_states.shape, F32),
            dma((OWNED + 1, 2)),
        ],
    )(retained, new_states)
    return retained, new_states.reshape(OWNED, 1, HEAD, HEAD)


def solution(mesh):
    return jax.shard_map(
        on_device,
        mesh=mesh,
        in_specs=(
            P("pool", "tp"),
            P(None, "tp"),
            P(None, "tp"),
            P(None, "tp"),
            P(None, "tp"),
            P("tp"),
            P("pool", "tp", None, None),
            P(),
            P(),
            P(),
        ),
        out_specs=(P("pool", "tp"), P("pool", "tp", None, None)),
        check_vma=False,
    )
```

```python
import functools

import jax
import jax.numpy as jnp
from jax import lax
from jax.experimental import pallas as pl
from jax.experimental.pallas import tpu as pltpu
from jax.sharding import PartitionSpec as P

MESH = pl.DeviceIdType.MESH
HEAD = 256
ROWS = 512
SESSIONS = 32
OWNED = 8
SLOTS = 4
LMAX = 128
SIZES = (256, 256)
CHUNKS = len(SIZES)
FIRST = tuple(sum(SIZES[:n]) for n in range(CHUNKS))
PART = 64
PARTS = ROWS // PART
SPAN = LMAX // PART + 1
BAND = 256
STAGGER = 4.5
EPSILON = 1e-05
F32 = jnp.float32
BF16 = jnp.bfloat16


def kernel(
    tokens, w_query, w_key, w_value, w_gate, pool, decay, lengths, slot_of, serve,
    retained, new_states, *scratch,
):
    lines = [scratch[4 * r:4 * r + 4] for r in range(CHUNKS)]
    scratch = scratch[4 * CHUNKS:]
    twins = [scratch[4 * r:4 * r + 4] for r in range(CHUNKS)]
    scratch = scratch[4 * CHUNKS:]
    prior, packed, keyval, scratch = scratch[:4], scratch[4:7], scratch[7:11], scratch[11:]
    total, scratch = scratch[:CHUNKS], scratch[CHUNKS:]
    (
        weights, prior_own, fresh, query, gate, starts,
        token_sem, pool_sem, weight_sem, out_sem,
        near_send, near_recv, near2_send, near2_recv, far_send, far_recv, far2_send, far2_recv,
        twin_send, twin_recv, state_send, state_recv, kv_send, kv_recv, relay_send, relay_recv,
    ) = scratch
    me = lax.axis_index("pool")
    place = lax.axis_index("tp")
    x, z, core = place // 8, (place // 2) % 4, place % 2
    u = x * (1 - core) + z * core
    v = z * (1 - core) + x * core

    def at(u_at, v_at):
        u_at, v_at = (u_at + 4) % 4, (v_at + 4) % 4
        x_at = u_at * (1 - core) + v_at * core
        z_at = v_at * (1 - core) + u_at * core
        return {"tp": x_at * 8 + z_at * 2 + core}

    twin = {"tp": x * 8 + z * 2 + (1 - core)}

    def group(offset):
        return {"pool": (me + offset + 4) % 4}

    def remote(src, dst, send, recv, device):
        return pltpu.make_async_remote_copy(
            src_ref=src, dst_ref=dst, send_sem=send, recv_sem=recv,
            device_id=device, device_id_type=MESH,
        )

    def rows_of(r):
        return pl.ds(FIRST[r], SIZES[r])

    partners = [at(u + 1, v), at(u - 1, v), at(u + 2, v), at(u, v + 1), at(u, v - 1)]
    partners += [twin] + [group(d) for d in (1, 2, 3)]
    barrier = pltpu.get_barrier_semaphore()
    for partner in partners:
        pl.semaphore_signal(barrier, inc=1, device_id=partner, device_id_type=MESH)

    token_copies = [
        pltpu.make_async_copy(
            tokens.at[rows_of(r)], lines[r][0].at[0], token_sem.at[r]
        )
        for r in range(CHUNKS)
    ]
    for copy in token_copies:
        copy.start()
    pool_copy = pltpu.make_async_copy(pool, prior_own, pool_sem)
    pool_copy.start()
    matrices = (w_query, w_key, w_value, w_gate)

    def weight_copy(plane, line, which):
        source = matrices[which]
        part = source.at[:, line, 0] if plane == 0 else source.at[line, :, 1]
        return pltpu.make_async_copy(
            part, weights.at[plane, line, which], weight_sem.at[plane, line, which]
        )

    def half(r, way):
        return pl.ds(way * (SIZES[r] // 2), SIZES[r] // 2)

    def near(r, way):
        return remote(
            lines[r][0].at[0], lines[r][0].at[1 + 2 * way],
            near_send.at[r, way], near_recv.at[r, way], at(u + 1 - 2 * way, v),
        )

    def near2(r):
        return remote(
            lines[r][0].at[0], lines[r][0].at[2], near2_send.at[r], near2_recv.at[r], at(u + 2, v)
        )

    def far(r, i, way):
        return remote(
            lines[r][0].at[i], lines[r][1 + 2 * way].at[i],
            far_send.at[r, i, way], far_recv.at[r, i, way], at(u, v + 1 - 2 * way),
        )

    def far2(r, i, way):
        return remote(
            lines[r][1 + 2 * way].at[i, half(r, way)], lines[r][2].at[i, half(r, way)],
            far2_send.at[r, i, way], far2_recv.at[r, i, way], at(u, v + 1 - 2 * way),
        )

    def to_twin(r, d, i):
        return remote(
            lines[r][d].at[i], twins[r][d].at[i], twin_send.at[r, d, i], twin_recv.at[r, d, i], twin
        )

    def spread(r, i):
        for way in range(2):
            far(r, i, way).start()
        to_twin(r, 0, i).start()

    def open_chunk(r):
        token_copies[r].wait()
        for way in range(2):
            near(r, way).start()
        near2(r).start()
        spread(r, 0)

    def near_in(r):
        for way in range(2):
            near(r, way).wait_recv()
            spread(r, 1 + 2 * way)

    def near2_in(r):
        near2(r).wait_recv()
        spread(r, 2)

    def far_in(r, i):
        for way in range(2):
            far(r, i, way).wait_recv()
            far2(r, i, way).start()
            to_twin(r, 1 + 2 * way, i).start()

    def far2_in(r, i):
        for way in range(2):
            far2(r, i, way).wait_recv()
        to_twin(r, 2, i).start()

    pl.semaphore_wait(barrier, len(partners))
    for r in range(CHUNKS):
        open_chunk(r)

    zero = jnp.int32(0)

    def scan(s, carry):
        own_rows, own_count, ids, id_count, run, inverse = carry
        slot, to, long = slot_of[s], serve[s], lengths[s]
        owner, row = slot // OWNED, slot % OWNED
        begin = zero
        new_run = []
        for g in range(4):
            begin = jnp.where(to == g, run[g], begin)
            new_run.append(run[g] + jnp.where(to == g, long, 0))
        starts[s] = begin
        mine, here = owner == me, to == me
        ahead, behind = (to - me + 4) % 4, (me - owner + 4) % 4
        own_rows_n, own_count_n, ids_n, id_count_n = [], [], [], []
        for g in range(4):
            hit = mine & (ahead == g)
            own_rows_n.append(jnp.where(hit, own_rows[g] * 8 + row, own_rows[g]))
            own_count_n.append(own_count[g] + jnp.where(hit, 1, 0))
            hit = here & (behind == g)
            ids_n.append(jnp.where(hit, ids[g] * 32 + s, ids[g]))
            id_count_n.append(id_count[g] + jnp.where(hit, 1, 0))
        return (
            tuple(own_rows_n), tuple(own_count_n), tuple(ids_n), tuple(id_count_n),
            tuple(new_run),
            tuple(jnp.where(mine & (row == i), s, inverse[i]) for i in range(OWNED)),
        )

    four = (zero,) * 4
    own_rows, _, ids, id_count, _, inverse = lax.fori_loop(
        0, SESSIONS, scan, (four, four, four, four, four, (zero,) * OWNED)
    )

    def state(d, k):
        return remote(
            packed[d - 1].at[k], prior[d].at[k],
            state_send.at[d - 1, k], state_recv.at[d - 1, k], group(d),
        )

    pool_copy.wait()
    for k in range(SLOTS):
        for d in (2, 1, 3):
            packed[d - 1][k] = prior_own[(own_rows[d] >> (3 * k)) & 7].astype(BF16)
            state(d, k).start()
    for k in range(SLOTS):
        prior[0][k] = prior_own[(own_rows[0] >> (3 * k)) & 7].astype(BF16)

    for line in range(4):
        for plane in range(2):
            for which in range(4):
                weight_copy(plane, line, which).start()

    def multiply(part, plane, line, first, r, pair):
        left = jnp.concatenate([part[i] for i in range(4)], axis=1)

        def one(n, _):
            which = 1 + n if pair == 0 else 3 * n
            right = jnp.concatenate(
                [weights[plane, line, which, (first - i + 4) % 4] for i in range(4)], axis=0
            )
            total[r][n] += jnp.dot(left, right, preferred_element_type=F32)
            return 0

        lax.fori_loop(0, 2, one, 0, unroll=True)

    def own(r, d, pair=0):
        multiply(lines[r][d], core, (v - d + 4) % 4, u, r, pair)

    def other(r, d, pair=0):
        if pair == 0:
            for i in range(4):
                to_twin(r, d, i).wait_recv()
        multiply(twins[r][d], 1 - core, (u - d + 4) % 4, v, r, pair)

    def side(way):
        return group(1 if way == 0 else -1)

    def parts_of(r):
        return pl.ds(FIRST[r] // PART, SIZES[r] // PART)

    def kv_out(r, way, which):
        return remote(
            keyval[0].at[which, parts_of(r)], keyval[1 + way].at[which, parts_of(r)],
            kv_send.at[r, way, which], kv_recv.at[r, way, which], side(way),
        )

    def relay(r, way):
        return remote(
            keyval[1 + way].at[way, parts_of(r)], keyval[3].at[way, parts_of(r)],
            relay_send.at[r, way], relay_recv.at[r, way], side(way),
        )

    def finish(r):
        shape = (SIZES[r] // PART, PART, HEAD)
        keyval[0][0, parts_of(r)] = (total[r][0] * HEAD ** (-0.5)).astype(BF16).reshape(shape)
        kv_out(r, 0, 0).start()
        keyval[0][1, parts_of(r)] = total[r][1].astype(BF16).reshape(shape)
        kv_out(r, 1, 1).start()
        kv_out(r, 0, 1).start()
        kv_out(r, 1, 0).start()

    def pass_on(r):
        for way in range(2):
            kv_out(r, way, way).wait_recv()
            relay(r, way).start()

    def rest(r):
        total[r][...] = jnp.zeros_like(total[r])
        for d in range(4):
            own(r, d, 1)
            other(r, d, 1)
        query[rows_of(r), :] = total[r][0].astype(BF16)
        gate[rows_of(r), :] = total[r][1].astype(BF16)

    def get_weights(_):
        for line in range(4):
            for plane in range(2):
                for which in range(4):
                    weight_copy(plane, line, which).wait()

    steps = [
        (1, near_in), (2, far_in, 0), (3, near2_in), (4, far_in, 1), (5, far_in, 3), (6, far_in, 2),
        (7, far2_in, 0), (8, far2_in, 1), (9, far2_in, 3), (10, far2_in, 2),
        (8.5, own, 0), (8.6, other, 0), (9.2, own, 1), (9.5, own, 3), (10.2, other, 1),
        (10.3, other, 3), (10.5, own, 2), (11, other, 2), (11.5, finish),
    ]
    for r in range(CHUNKS):
        total[r][...] = jnp.zeros_like(total[r])
    order = [(when + STAGGER * r, r, *step) for r in range(CHUNKS) for when, *step in steps]
    order.append((6.4, 0, get_weights))
    order += [(15.1 + STAGGER * r, r, pass_on) for r in range(CHUNKS - 1)]
    for _, r, step, *more in sorted(order, key=lambda entry: entry[:2]):
        step(r, *more)
    rest(0)
    pass_on(CHUNKS - 1)
    for r in range(1, CHUNKS):
        rest(r)

    for k in range(SLOTS):
        for d in (1, 2, 3):
            state(d, k).wait_recv()

    log_gamma = jnp.log(jnp.full((1, 1), decay[0], F32))

    first, last = [], []
    for g in range(4):
        for k in range(SLOTS):
            s = (ids[g] >> (5 * k)) & 31
            first.append(starts[s])
            last.append(jnp.where(k < id_count[g], starts[s] + lengths[s], 0))

    def own_rows_of(which):
        return keyval[0][which].reshape(ROWS, HEAD)

    def retain(r, _):
        rows = pl.ds(pl.multiple_of(r * BAND, BAND), BAND)
        row = lax.broadcasted_iota(jnp.int32, (BAND, 1), 0) + r * BAND
        begin = jnp.full((BAND, 1), ROWS, jnp.int32)
        q = query[rows, :]
        carried = jnp.zeros((BAND, HEAD), F32)
        for g in range(4):
            parts = []
            for k in range(SLOTS):
                n = g * SLOTS + k
                inside = (row >= first[n]) & (row < last[n])
                begin = jnp.where(inside, first[n], begin)
                parts.append(jnp.where(inside, q, jnp.zeros_like(q)))
            carried += jnp.dot(
                jnp.concatenate(parts, axis=1), prior[g][...].reshape(SLOTS * HEAD, HEAD),
                preferred_element_type=F32,
            )
        live = begin < ROWS
        column = lax.broadcasted_iota(jnp.int32, (BAND, ROWS), 1)
        distance = row - column
        scores = lax.dot_general(
            q, own_rows_of(0), (((1,), (1,)), ((), ())), preferred_element_type=F32
        )
        weight = jnp.exp(jnp.maximum(distance, 0).astype(F32) * log_gamma)
        mixing = jnp.where((distance >= 0) & (column >= begin), scores * weight, 0.0).astype(BF16)
        mixed = jnp.dot(
            mixing, own_rows_of(1), preferred_element_type=F32
        )
        reach = jnp.exp(jnp.maximum(row - begin + 1, 0).astype(F32) * log_gamma)
        mixed = mixed + carried * jnp.where(live, reach, 0.0)
        centered = mixed - jnp.mean(mixed, axis=-1, keepdims=True)
        variance = jnp.mean(centered * centered, axis=-1, keepdims=True)
        normed = centered * lax.rsqrt(variance + EPSILON)
        out = gate[rows, :].astype(F32)
        out = out * (1.0 / (1.0 + jnp.exp(-out))) * normed
        retained[rows, :] = jnp.where(live, out, 0.0).astype(BF16)
        return 0

    lax.fori_loop(0, ROWS // BAND, retain, 0)
    for r in range(CHUNKS):
        for way in range(2):
            kv_out(r, way, 1 - way).wait_recv()
    for r in range(CHUNKS):
        for way in range(2):
            relay(r, way).wait_recv()
    out_copies = []
    for i in range(OWNED):
        s = inverse[i]
        begin, long = starts[s], lengths[s]
        away = (me - serve[s] + 4) % 4
        low = jnp.minimum(begin // PART, PARTS - SPAN)
        row = lax.broadcasted_iota(jnp.int32, (SPAN * PART, 1), 0) + low * PART
        behind = begin + long - 1 - row
        tail = jnp.exp(jnp.maximum(behind, 0).astype(F32) * log_gamma)
        tail = jnp.where((row >= begin) & (behind >= 0), tail, 0.0)

        def turn_rows(which):
            blocks = []
            for n in range(SPAN):
                block = keyval[0][which, low + n]
                for place, group_away in ((1, 1), (2, 3), (3, 2)):
                    block = jnp.where(away == group_away, keyval[place][which, low + n], block)
                blocks.append(block)
            return jnp.concatenate(blocks, axis=0)

        change = lax.dot_general(
            (turn_rows(0).astype(F32) * tail).astype(BF16), turn_rows(1),
            (((0,), (0,)), ((), ())), preferred_element_type=F32,
        )
        keep = jnp.exp(jnp.full((1, 1), long, jnp.int32).astype(F32) * log_gamma)
        fresh[i] = keep * prior_own[i] + change
        out_copies.append(pltpu.make_async_copy(fresh.at[i], new_states.at[i], out_sem.at[i]))
        out_copies[i].start()
    for r in range(CHUNKS):
        for i in range(4):
            for d in range(4):
                to_twin(r, d, i).wait_send()
            for way in range(2):
                far(r, i, way).wait_send()
                far2(r, i, way).wait_send()
        near2(r).wait_send()
        for way in range(2):
            near(r, way).wait_send()
            for which in range(2):
                kv_out(r, way, which).wait_send()
            relay(r, way).wait_send()
    for k in range(SLOTS):
        for d in (1, 2, 3):
            state(d, k).wait_send()
    for copy in out_copies:
        copy.wait()


def deliver(retained, new_states, retained_out, new_states_out, rows, states, sem):
    passes = [(retained, rows, retained_out)]
    passes += [(new_states.at[i], states.at[i], new_states_out.at[i]) for i in range(OWNED)]
    loads = [
        pltpu.make_async_copy(src, held, sem.at[n, 0]) for n, (src, held, _) in enumerate(passes)
    ]
    stores = [
        pltpu.make_async_copy(held, dst, sem.at[n, 1]) for n, (_, held, dst) in enumerate(passes)
    ]
    for load in loads:
        load.start()
    for load, store in zip(loads, stores):
        load.wait()
        store.start()
    for store in stores:
        store.wait()


def on_device(tokens, w_query, w_key, w_value, w_gate, decay, pool_states, lengths, slot_of, serve):
    hbm = pl.BlockSpec(memory_space=pl.ANY)
    vmem = pl.BlockSpec(memory_space=pltpu.VMEM)
    smem = pl.BlockSpec(memory_space=pltpu.SMEM)
    dma = pltpu.SemaphoreType.DMA
    split = [w.reshape(4, 4, 2, HEAD, HEAD) for w in (w_query, w_key, w_value, w_gate)]
    states = pool_states.reshape(OWNED, HEAD, HEAD)
    retained, new_states = pl.pallas_call(
        kernel,
        out_shape=(
            jax.ShapeDtypeStruct((ROWS, HEAD), BF16),
            jax.ShapeDtypeStruct((OWNED, HEAD, HEAD), F32),
        ),
        in_specs=[hbm] * 6 + [smem] * 4,
        out_specs=(vmem, hbm),
        scratch_shapes=[
            *[pltpu.VMEM((4, size, HEAD), BF16) for size in SIZES for _ in range(4)] * 2,
            *[pltpu.VMEM((SLOTS, HEAD, HEAD), BF16)] * 7,
            *[pltpu.VMEM((2, PARTS, PART, HEAD), BF16)] * 4,
            *[pltpu.VMEM((2, size, HEAD), F32) for size in SIZES],
            pltpu.VMEM((2, 4, 4, 4, HEAD, HEAD), BF16),
            *[pltpu.VMEM((OWNED, HEAD, HEAD), F32)] * 2,
            pltpu.VMEM((ROWS, HEAD), BF16),
            pltpu.VMEM((ROWS, HEAD), BF16),
            pltpu.SMEM((SESSIONS,), jnp.int32),
            dma((CHUNKS,)), dma, dma((2, 4, 4)), dma((OWNED,)),
            *[dma((CHUNKS, 2))] * 2,
            *[dma((CHUNKS,))] * 2,
            *[dma((CHUNKS, 4, 2))] * 4,
            *[dma((CHUNKS, 4, 4))] * 2,
            dma((3, SLOTS)), dma((3, SLOTS)),
            dma((CHUNKS, 2, 2)), dma((CHUNKS, 2, 2)),
            dma((CHUNKS, 2)), dma((CHUNKS, 2)),
        ],
        compiler_params=pltpu.CompilerParams(
            collective_id=0, has_side_effects=True, vmem_limit_bytes=56 << 20
        ),
        cost_estimate=pl.CostEstimate(
            flops=11_000_000_000, bytes_accessed=24_000_000, transcendentals=1_000_000
        ),
    )(tokens, *split, states, decay, lengths, slot_of, serve)
    retained, new_states = pl.pallas_call(
        deliver,
        out_shape=(
            jax.ShapeDtypeStruct(retained.shape, BF16),
            jax.ShapeDtypeStruct(new_states.shape, F32),
        ),
        in_specs=[hbm, hbm],
        out_specs=(hbm, hbm),
        scratch_shapes=[
            pltpu.VMEM(retained.shape, BF16),
            pltpu.VMEM(new_states.shape, F32),
            dma((OWNED + 1, 2)),
        ],
    )(retained, new_states)
    return retained, new_states.reshape(OWNED, 1, HEAD, HEAD)


def solution(mesh):
    return jax.shard_map(
        on_device,
        mesh=mesh,
        in_specs=(
            P("pool", "tp"),
            P(None, "tp"),
            P(None, "tp"),
            P(None, "tp"),
            P(None, "tp"),
            P("tp"),
            P("pool", "tp", None, None),
            P(),
            P(),
            P(),
        ),
        out_specs=(P("pool", "tp"), P("pool", "tp", None, None)),
        check_vma=False,
    )
```
